512 devices in a mesh: ctx: 64 (over y, x, core), cand: 8 (over z).
Axes of the slice: x: 4, y: 8, z: 8, core: 2. Of those that a mesh axis runs over, the one named last changes fastest.
Arguments:
- memory: bfloat16 [16384, 8192], P('ctx', 'cand'), may hold values from -60 to 60
- kv_weight: bfloat16 [2048, 8192], P('ctx', 'cand'), may hold values from -0.06629126 to 0.06629126
- queries: bfloat16 [512, 8192], P('cand', 'ctx'), may hold values from -64 to 64
Outputs:
- attended: bfloat16 [512, 8192], P('cand', 'ctx')
The draws below stay inside these ranges and needn't reach their ends.
All inputs are finite; a program needn't handle non-finite values.
Results may differ from the reference program's by a relative error of at most 0.012.
The reference program's roundings to bfloat16 on the way (of `kv` and `weights`) count: a program that leaves them out, or rounds other values in their place, can miss the bound.
Values may be sent and summed in bfloat16 or wider, within the bound.
No kernel may reach another device: no remote copies, remote signals or barrier semaphores. Data moves between devices by JAX's collectives and lax.ppermute only.
A program may use at most 64 MiB of HBM per device.

```python
import jax
import jax.numpy as jnp
from jax import lax

D = 8192
QH = 64
KVH = 8
HD = 128
TOK_DEV = 256
TOKENS = 16384
CAND = 512
N_CTX = 64


def shared_arrays(key, row_top):
    key_mem = jax.random.fold_in(key, 101)
    key_scale = jax.random.fold_in(key, 102)
    key_weight = jax.random.fold_in(key, 103)
    gauss = jnp.clip(jax.random.normal(key_mem, (TOKENS, D), jnp.float32), -6.0, 6.0)
    base = gauss
    scales = jnp.exp(jax.random.uniform(key_scale, (TOKENS, 1), jnp.float32, 0.0, 1.0) * jnp.log(row_top))
    memory = base * scales
    weight = jnp.clip(jax.random.normal(key_weight, (2 * KVH * HD, D), jnp.float32), -6.0, 6.0) * D ** (-0.5)
    return (memory, weight)


def draw_memory(key, part):
    memory, weight = shared_arrays(key, 1.0)
    return memory.astype(jnp.bfloat16)


def draw_kv_weight(key, part):
    memory, weight = shared_arrays(key, 1.0)
    return weight.astype(jnp.bfloat16)


def draw_queries(key, part):
    key = jax.random.fold_in(key, 7)
    result = jnp.clip(jax.random.normal(key, (CAND, QH * HD), jnp.float32) * 2.5, -15.0, 15.0)
    return result.astype(jnp.bfloat16)


def setup_inputs(seed: int = 0) -> dict:
    seeds = jax.random.split(jax.random.key(seed), 4)
    return {
        "memory": draw_memory(jax.random.fold_in(seeds[3], 71), 0),
        "kv_weight": draw_kv_weight(jax.random.fold_in(seeds[3], 71), 0),
        "queries": draw_queries(jax.random.fold_in(seeds[3], 71), 0),
    }


def reference(memory, kv_weight, queries):
    kv = lax.dot_general(memory, kv_weight, (((1,), (1,)), ((), ())), preferred_element_type=jnp.float32).astype(jnp.bfloat16)
    keys = kv[:, :KVH * HD].reshape(TOKENS, KVH, HD)
    values = kv[:, KVH * HD:].reshape(TOKENS, KVH, HD)
    query_all = queries.reshape(CAND, QH, HD)
    group = QH // KVH

    def one_head(head):
        kv_head = head // group
        query = lax.dynamic_index_in_dim(query_all, head, 1, keepdims=False)
        key_head = lax.dynamic_index_in_dim(keys, kv_head, 1, keepdims=False)
        value_head = lax.dynamic_index_in_dim(values, kv_head, 1, keepdims=False)
        scores = jnp.dot(query, key_head.T, preferred_element_type=jnp.float32) * (HD ** -0.5)
        scores = scores.reshape(CAND, N_CTX, TOK_DEV)
        block_max = jnp.max(scores, axis=2)
        expo = jnp.exp(scores - block_max[:, :, None])
        block_total = jnp.sum(expo, axis=2)
        weights = expo.astype(jnp.bfloat16)
        block_out = jnp.einsum("cbt,btd->cbd", weights.astype(jnp.float32), value_head.reshape(N_CTX, TOK_DEV, HD).astype(jnp.float32))
        top = jnp.max(block_max, axis=1)
        factor = jnp.exp(block_max - top[:, None])
        numer = jnp.sum(factor[:, :, None] * block_out, axis=1)
        denom = jnp.sum(factor * block_total, axis=1)
        return (numer / denom[:, None]).astype(jnp.bfloat16)

    heads = lax.map(one_head, jnp.arange(QH, dtype=jnp.int32))
    return jnp.transpose(heads, (1, 0, 2)).reshape(CAND, QH * HD)
```

```python
import jax
import jax.numpy as jnp
from jax import lax
from jax.experimental import pallas as pl
from jax.experimental.pallas import tpu as pltpu
from jax.sharding import Mesh, PartitionSpec as P

HD = 128
NT = (((1,), (1,)), ((), ()))
NN = (((1,), (0,)), ((), ()))


def spread(value, axis):
    count = lax.axis_size(axis)
    copies = jnp.broadcast_to(value[None], (count,) + value.shape)
    return lax.all_to_all(copies, axis, 0, 0, tiled=True)


def place(y, x, c, z):
    return ((y * 4 + x) * 2 + c) * 8 + z


def weight_moves():
    moves = []
    for y in range(8):
        for x in range(4):
            for c in range(2):
                shard = y * 8 + x * 2 + c
                kind, head, quarter = shard // 32, shard // 4 % 8, shard % 4
                for z in range(8):
                    moves.append((place(y, x, c, z), place(kind * 4 + quarter, z // 2, z % 2, head)))
    return moves


def query_moves():
    return [
        (place(y, x, c, z), place(x * 2 + c, z // 2, z % 2, y))
        for y in range(8)
        for x in range(4)
        for c in range(2)
        for z in range(8)
    ]


ALL = ("y", "x", "c", "z")
RIGHT = [(i, (i + 1) % 4) for i in range(4)]
LEFT = [(i, (i - 1) % 4) for i in range(4)]
SWAP = [(0, 1), (1, 0)]


def project_kernel(core_ref, mem_a, mem_b, w_a, w_b, out_ref, acc):
    step = pl.program_id(0)
    part = lax.dot_general(mem_a[...], w_a[...], NT, preferred_element_type=jnp.float32)
    part += lax.dot_general(mem_b[...], w_b[...], NT, preferred_element_type=jnp.float32)

    @pl.when(step == 0)
    def _():
        acc[...] = part

    @pl.when(step > 0)
    def _():
        acc[...] += part

    @pl.when(step == pl.num_programs(0) - 1)
    def _():
        out_ref[...] = acc[...].astype(out_ref.dtype)


def project(core, mem_all, w_a, w_b):
    tok, feat = 256, mem_all.shape[1]
    return pl.pallas_call(
        project_kernel,
        out_shape=jax.ShapeDtypeStruct((tok, 2 * HD), jnp.bfloat16),
        grid_spec=pltpu.PrefetchScalarGridSpec(
            num_scalar_prefetch=1,
            grid=(4,),
            in_specs=[
                pl.BlockSpec((tok, feat), lambda j, core: (2 * j + core[0], 0)),
                pl.BlockSpec((tok, feat), lambda j, core: (2 * j + 1 - core[0], 0)),
                pl.BlockSpec((2 * HD, feat), lambda j, core: (j, 0)),
                pl.BlockSpec((2 * HD, feat), lambda j, core: (j, 0)),
            ],
            out_specs=pl.BlockSpec((tok, 2 * HD), lambda j, core: (0, 0)),
            scratch_shapes=[pltpu.VMEM((tok, 2 * HD), jnp.float32)],
        ),
        compiler_params=pltpu.CompilerParams(vmem_limit_bytes=24 << 20),
        cost_estimate=pl.CostEstimate(flops=2 * 256 * 256 * 8192, bytes_accessed=8 << 20, transcendentals=0),
    )(core, mem_all, mem_all, w_a, w_b)


def attend_kernel(q_ref, own, other, left, right, opp_a, opp_b, out_ref):
    blocks = [(own, 0), (other, 0), (left, 0), (left, 256), (right, 0), (right, 256), (opp_a, 0), (opp_b, 0)]
    query = q_ref[...]
    top = total = acc = None
    for ref, start in blocks:
        keys = ref[start : start + 256, :HD]
        values = ref[start : start + 256, HD:]
        scores = lax.dot_general(query, keys, NT, preferred_element_type=jnp.float32) * HD ** (-0.5)
        block_max = jnp.max(scores, axis=1, keepdims=True)
        expo = jnp.exp(scores - block_max)
        block_total = jnp.sum(expo, axis=1, keepdims=True)
        block_out = lax.dot_general(expo.astype(jnp.bfloat16), values, NN, preferred_element_type=jnp.float32)
        if top is None:
            top, total, acc = block_max, block_total, block_out
        else:
            new_top = jnp.maximum(top, block_max)
            keep, add = jnp.exp(top - new_top), jnp.exp(block_max - new_top)
            total = total * keep + block_total * add
            acc = acc * keep + block_out * add
            top = new_top
    tops = jnp.concatenate([top[h * 64 : h * 64 + 64] for h in range(8)], axis=1)
    totals = jnp.concatenate([total[h * 64 : h * 64 + 64] for h in range(8)], axis=1)
    stats = jnp.concatenate([tops, totals], axis=0).T
    for h in range(8):
        out_ref[h, :64, :] = acc[h * 64 : h * 64 + 64]
        out_ref[h, 64:, :] = jnp.broadcast_to(stats[h : h + 1], (8, HD))


def attend(query, pieces):
    return pl.pallas_call(
        attend_kernel,
        out_shape=jax.ShapeDtypeStruct((8, 72, HD), jnp.float32),
        compiler_params=pltpu.CompilerParams(vmem_limit_bytes=24 << 20),
        cost_estimate=pl.CostEstimate(
            flops=4 * 512 * 2048 * HD, bytes_accessed=2 << 20, transcendentals=512 * 2048
        ),
    )(query, *pieces)


def merge_kernel(part_ref, out_ref):
    stats = jnp.concatenate([part_ref[j, 64:65, :] for j in range(8)], axis=0).T
    tops, totals = stats[:64], stats[64:]
    top = jnp.max(tops, axis=1, keepdims=True)
    factor = jnp.exp(tops - top)
    denom = jnp.sum(factor * totals, axis=1, keepdims=True)
    numer = factor[:, :1] * part_ref[0, :64, :]
    for j in range(1, 8):
        numer += factor[:, j : j + 1] * part_ref[j, :64, :]
    out_ref[...] = (numer / denom).astype(out_ref.dtype)


def merge(parts):
    return pl.pallas_call(
        merge_kernel,
        out_shape=jax.ShapeDtypeStruct((64, HD), jnp.bfloat16),
    )(parts)


def body(memory, kv_weight, queries):
    core = lax.axis_index("c")
    mem_all = lax.all_gather(memory, "z", axis=0, tiled=True)

    rows = lax.ppermute(kv_weight, ALL, weight_moves())
    query = lax.ppermute(queries, ALL, query_moves())
    rows = spread(rows, "y").reshape(2 * HD, -1)
    w_a = spread(rows, "x").reshape(8 * HD, -1)
    w_b = lax.ppermute(w_a, "c", SWAP)
    query = spread(query, "y").reshape(512, HD)

    own = project(core.astype(jnp.int32)[None], mem_all, w_a, w_b)
    other = lax.ppermute(own, "c", SWAP)
    pair = jnp.concatenate([own, other], axis=0)
    left = lax.ppermute(pair, "x", RIGHT)
    right = lax.ppermute(pair, "x", LEFT)
    opp_a = lax.ppermute(left[:256], "x", RIGHT)
    opp_b = lax.ppermute(right[256:], "x", LEFT)

    parts = attend(query, (own, other, left, right, opp_a, opp_b))
    parts = lax.all_to_all(parts, "y", 0, 0, tiled=True)
    result = merge(parts)
    return lax.ppermute(result, ALL, [(b, a) for a, b in query_moves()])


def solution(mesh):
    fine = Mesh(mesh.devices.reshape(8, 4, 2, 8), ALL)
    ctx = ("y", "x", "c")
    return jax.shard_map(
        body,
        mesh=fine,
        in_specs=(P(ctx, "z"), P(ctx, "z"), P("z", ctx)),
        out_specs=P("z", ctx),
        check_vma=False,
    )
```

```python
import jax
import jax.numpy as jnp
from jax import lax
from jax.experimental import pallas as pl
from jax.experimental.pallas import tpu as pltpu
from jax.sharding import Mesh, PartitionSpec as P

HD = 128
NT = (((1,), (1,)), ((), ()))
NN = (((1,), (0,)), ((), ()))


def spread(value, axis):
    count = lax.axis_size(axis)
    copies = jnp.broadcast_to(value[None], (count,) + value.shape)
    return lax.all_to_all(copies, axis, 0, 0, tiled=True)


def place(y, x, c, z):
    return ((y * 4 + x) * 2 + c) * 8 + z


def weight_moves():
    moves = []
    for y in range(8):
        for x in range(4):
            for c in range(2):
                shard = y * 8 + x * 2 + c
                kind, head, quarter = shard // 32, shard // 4 % 8, shard % 4
                for z in range(8):
                    moves.append((place(y, x, c, z), place(kind * 4 + quarter, z // 2, z % 2, head)))
    return moves


def query_moves():
    return [
        (place(y, x, c, z), place(z, x, c, y)) for y in range(8) for x in range(4) for c in range(2) for z in range(8)
    ]


ALL = ("y", "x", "c", "z")
def shift(count, away):
    return [(i, (i + away) % count) for i in range(count)]


SWAP = [(0, 1), (1, 0)]


def project_kernel(*refs):
    mem, mem_a, mem_b, w_refs, (out_ref, held, sems) = refs[:7], refs[7], refs[8], refs[9:19], refs[19:]
    x, core, z = lax.axis_index("x"), lax.axis_index("c"), lax.axis_index("z")
    copies = []
    for swapped in range(2):
        half = core if swapped == 0 else 1 - core
        own, left, right, opp_k, opp_v = w_refs[5 * swapped : 5 * swapped + 5]
        for away, ref in ((0, own), (3, left), (1, right)):
            copies.append((ref, held.at[lax.rem(x + away, 4) * 2 + half]))
        opposite = lax.rem(x + 2, 4) * 2 + half
        copies.append((opp_k, held.at[opposite, pl.ds(0, HD)]))
        copies.append((opp_v, held.at[opposite, pl.ds(HD, HD)]))
    copies = [pltpu.make_async_copy(src, dst, sems.at[j]) for j, (src, dst) in enumerate(copies)]
    for copy in copies:
        copy.start()
    for copy in copies:
        copy.wait()
    total = None
    for ref, away in zip(mem, (0, 7, 6, 5, 1, 2, 3)):
        w_rows = held[lax.rem(z + away, 8)]
        part = lax.dot_general(ref[...], w_rows, NT, preferred_element_type=jnp.float32)
        total = part if total is None else total + part
    w_rows = held[lax.rem(z + 4, 8)]
    for start, ref in ((0, mem_a), (128, mem_b)):
        part = lax.dot_general(ref[...], w_rows, NT, preferred_element_type=jnp.float32)
        out_ref[start : start + 128] = (total[start : start + 128] + part).astype(out_ref.dtype)


def project(mem, w_pieces):
    vmem = pl.BlockSpec(memory_space=pltpu.VMEM)
    return pl.pallas_call(
        project_kernel,
        out_shape=jax.ShapeDtypeStruct((256, 2 * HD), jnp.bfloat16),
        in_specs=[vmem] * 9 + [pl.BlockSpec(memory_space=pl.ANY)] * 10,
        out_specs=vmem,
        scratch_shapes=[pltpu.VMEM((8, 2 * HD, 8 * HD), jnp.bfloat16), pltpu.SemaphoreType.DMA((10,))],
        compiler_params=pltpu.CompilerParams(vmem_limit_bytes=24 << 20),
        cost_estimate=pl.CostEstimate(flops=2 * 256 * 256 * 8192, bytes_accessed=8 << 20, transcendentals=0),
    )(*mem, *w_pieces)


def attend_kernel(q_ref, own, other, out_ref):
    blocks = [(ref, start) for ref in (own, other) for start in range(0, 1024, 256)]
    query = q_ref[...]
    top = total = acc = None
    for ref, start in blocks:
        keys = ref[start : start + 256, :HD]
        values = ref[start : start + 256, HD:]
        scores = lax.dot_general(query, keys, NT, preferred_element_type=jnp.float32) * HD ** (-0.5)
        block_max = jnp.max(scores, axis=1, keepdims=True)
        expo = jnp.exp(scores - block_max)
        block_total = jnp.sum(expo, axis=1, keepdims=True)
        block_out = lax.dot_general(expo.astype(jnp.bfloat16), values, NN, preferred_element_type=jnp.float32)
        if top is None:
            top, total, acc = block_max, block_total, block_out
        else:
            new_top = jnp.maximum(top, block_max)
            keep, add = jnp.exp(top - new_top), jnp.exp(block_max - new_top)
            total = total * keep + block_total * add
            acc = acc * keep + block_out * add
            top = new_top
    tops = jnp.concatenate([top[h * 64 : h * 64 + 64] for h in range(8)], axis=1)
    totals = jnp.concatenate([total[h * 64 : h * 64 + 64] for h in range(8)], axis=1)
    stats = jnp.concatenate([tops, totals], axis=0).T
    for h in range(8):
        out_ref[h, :64, :] = acc[h * 64 : h * 64 + 64]
        out_ref[h, 64:, :] = jnp.broadcast_to(stats[h : h + 1], (8, HD))


def attend(query, own, other):
    return pl.pallas_call(
        attend_kernel,
        out_shape=jax.ShapeDtypeStruct((8, 72, HD), jnp.float32),
        compiler_params=pltpu.CompilerParams(vmem_limit_bytes=24 << 20),
        cost_estimate=pl.CostEstimate(
            flops=4 * 512 * 2048 * HD, bytes_accessed=2 << 20, transcendentals=512 * 2048
        ),
    )(query, own, other)


def merge_kernel(part_ref, out_ref):
    stats = jnp.concatenate([part_ref[j, 64:65, :] for j in range(8)], axis=0).T
    tops, totals = stats[:64], stats[64:]
    top = jnp.max(tops, axis=1, keepdims=True)
    factor = jnp.exp(tops - top)
    denom = jnp.sum(factor * totals, axis=1, keepdims=True)
    numer = factor[:, :1] * part_ref[0, :64, :]
    for j in range(1, 8):
        numer += factor[:, j : j + 1] * part_ref[j, :64, :]
    out_ref[...] = (numer / denom).astype(out_ref.dtype)


def merge(parts):
    return pl.pallas_call(
        merge_kernel,
        out_shape=jax.ShapeDtypeStruct((64, HD), jnp.bfloat16),
    )(parts)


def ring(value):
    half = value.shape[0] // 2
    left = lax.ppermute(value, "x", shift(4, 1))
    right = lax.ppermute(value, "x", shift(4, -1))
    opp_a = lax.ppermute(left[:half], "x", shift(4, 1))
    opp_b = lax.ppermute(right[half:], "x", shift(4, -1))
    return value, left, right, opp_a, opp_b


def ring_z(value, after):
    ups = [lax.ppermute(value, "z", shift(8, 1))]
    downs = [lax.ppermute(value, "z", shift(8, -1))]
    ups[0], downs[0], after = lax.optimization_barrier((ups[0], downs[0], after))
    for _ in range(2):
        ups.append(lax.ppermute(ups[-1], "z", shift(8, 1)))
        downs.append(lax.ppermute(downs[-1], "z", shift(8, -1)))
    opp_a = lax.ppermute(ups[2][:128], "z", shift(8, 1))
    opp_b = lax.ppermute(downs[2][128:], "z", shift(8, -1))
    return (value, *ups, *downs, opp_a, opp_b), after


def swap(value):
    return lax.ppermute(value, "c", SWAP)


def body(memory, kv_weight, queries):
    rows = lax.ppermute(kv_weight, ALL, weight_moves())
    query = lax.ppermute(queries, ALL, query_moves())
    both = jnp.concatenate([rows, query.reshape(8, 8 * HD)], axis=0)
    mem, both = ring_z(memory, both)
    both = spread(both, "y")
    rows = both[:, :32].reshape(2 * HD, 8 * HD)
    query = both[:, 32:].reshape(512, HD)
    w_pieces = ring(rows)
    own = project(mem, (*w_pieces, *map(swap, w_pieces)))

    own = lax.all_gather(own, "x", axis=0, tiled=True)
    parts = attend(query, own, swap(own))
    parts = lax.all_to_all(parts, "y", 0, 0, tiled=True)
    result = merge(parts)
    return lax.ppermute(result, ALL, query_moves())


def solution(mesh):
    fine = Mesh(mesh.devices.reshape(8, 4, 2, 8), ALL)
    ctx = ("y", "x", "c")
    return jax.shard_map(
        body,
        mesh=fine,
        in_specs=(P(ctx, "z"), P(ctx, "z"), P("z", ctx)),
        out_specs=P("z", ctx),
        check_vma=False,
    )
```

```python
import jax
import jax.numpy as jnp
from jax import lax
from jax.experimental import pallas as pl
from jax.experimental.pallas import tpu as pltpu
from jax.sharding import Mesh, PartitionSpec as P

HD = 128
NT = (((1,), (1,)), ((), ()))
NN = (((1,), (0,)), ((), ()))


def spread(value, axis):
    count = lax.axis_size(axis)
    copies = jnp.broadcast_to(value[None], (count,) + value.shape)
    return lax.all_to_all(copies, axis, 0, 0, tiled=True)


def place(y, x, c, z):
    return ((y * 4 + x) * 2 + c) * 8 + z


def weight_moves():
    moves = []
    for y in range(8):
        for x in range(4):
            for c in range(2):
                shard = y * 8 + x * 2 + c
                kind, head, quarter = shard // 32, shard // 4 % 8, shard % 4
                for z in range(8):
                    moves.append((place(y, x, c, z), place(kind * 4 + quarter, z // 2, z % 2, head)))
    return moves


def query_moves():
    return [
        (place(y, x, c, z), place(z, x, c, y)) for y in range(8) for x in range(4) for c in range(2) for z in range(8)
    ]


ALL = ("y", "x", "c", "z")
def shift(count, away):
    return [(i, (i + away) % count) for i in range(count)]


SWAP = [(0, 1), (1, 0)]


def project_kernel(*refs):
    mem, (mem_a, mem_b, w_a, w_b, out_ref) = refs[:7], refs[7:]
    core, z = lax.axis_index("c"), lax.axis_index("z")

    def run(even, odd):
        def rows(away):
            return (even, odd)[away % 2][lax.rem(z + away, 8) // 2]

        total = None
        for ref, away in zip(mem, (0, 7, 6, 5, 1, 2, 3)):
            part = lax.dot_general(ref[...], rows(away), NT, preferred_element_type=jnp.float32)
            total = part if total is None else total + part
        for start, ref in ((0, mem_a), (128, mem_b)):
            part = lax.dot_general(ref[...], rows(4), NT, preferred_element_type=jnp.float32)
            out_ref[start : start + 128] = (total[start : start + 128] + part).astype(out_ref.dtype)

    @pl.when(lax.rem(z, 2) == core)
    def _():
        run(w_a, w_b)

    @pl.when(lax.rem(z, 2) != core)
    def _():
        run(w_b, w_a)


def project(mem, w_a, w_b):
    return pl.pallas_call(
        project_kernel,
        out_shape=jax.ShapeDtypeStruct((256, 2 * HD), jnp.bfloat16),
        compiler_params=pltpu.CompilerParams(vmem_limit_bytes=32 << 20),
        cost_estimate=pl.CostEstimate(flops=2 * 256 * 256 * 8192, bytes_accessed=8 << 20, transcendentals=0),
    )(*mem, w_a, w_b)


def attend_kernel(q_ref, own, other, out_ref):
    blocks = [(ref, start) for ref in (own, other) for start in range(0, 1024, 256)]
    query = q_ref[...]
    top = total = acc = None
    for ref, start in blocks:
        keys = ref[start : start + 256, :HD]
        values = ref[start : start + 256, HD:]
        scores = lax.dot_general(query, keys, NT, preferred_element_type=jnp.float32) * HD ** (-0.5)
        block_max = jnp.max(scores, axis=1, keepdims=True)
        expo = jnp.exp(scores - block_max)
        block_total = jnp.sum(expo, axis=1, keepdims=True)
        block_out = lax.dot_general(expo.astype(jnp.bfloat16), values, NN, preferred_element_type=jnp.float32)
        if top is None:
            top, total, acc = block_max, block_total, block_out
        else:
            new_top = jnp.maximum(top, block_max)
            keep, add = jnp.exp(top - new_top), jnp.exp(block_max - new_top)
            total = total * keep + block_total * add
            acc = acc * keep + block_out * add
            top = new_top
    tops = jnp.concatenate([top[h * 64 : h * 64 + 64] for h in range(8)], axis=1)
    totals = jnp.concatenate([total[h * 64 : h * 64 + 64] for h in range(8)], axis=1)
    stats = jnp.concatenate([tops, totals], axis=0).T
    for h in range(8):
        out_ref[h, :64, :] = acc[h * 64 : h * 64 + 64]
        out_ref[h, 64:, :] = jnp.broadcast_to(stats[h : h + 1], (8, HD))


def attend(query, own, other):
    return pl.pallas_call(
        attend_kernel,
        out_shape=jax.ShapeDtypeStruct((8, 72, HD), jnp.float32),
        compiler_params=pltpu.CompilerParams(vmem_limit_bytes=24 << 20),
        cost_estimate=pl.CostEstimate(
            flops=4 * 512 * 2048 * HD, bytes_accessed=2 << 20, transcendentals=512 * 2048
        ),
    )(query, own, other)


def merge_kernel(part_ref, out_ref):
    stats = jnp.concatenate([part_ref[j, 64:65, :] for j in range(8)], axis=0).T
    tops, totals = stats[:64], stats[64:]
    top = jnp.max(tops, axis=1, keepdims=True)
    factor = jnp.exp(tops - top)
    denom = jnp.sum(factor * totals, axis=1, keepdims=True)
    numer = factor[:, :1] * part_ref[0, :64, :]
    for j in range(1, 8):
        numer += factor[:, j : j + 1] * part_ref[j, :64, :]
    out_ref[...] = (numer / denom).astype(out_ref.dtype)


def merge(parts):
    return pl.pallas_call(
        merge_kernel,
        out_shape=jax.ShapeDtypeStruct((64, HD), jnp.bfloat16),
    )(parts)


def step_z(ups, downs):
    return lax.ppermute(ups, "z", shift(8, 1)), lax.ppermute(downs, "z", shift(8, -1))


def swap(value):
    return lax.ppermute(value, "c", SWAP)


def body(memory, kv_weight, queries):
    rows = lax.ppermute(kv_weight, ALL, weight_moves())
    query = lax.ppermute(queries, ALL, query_moves())
    memory, rows, query = lax.optimization_barrier((memory, rows, query))
    both = spread(jnp.concatenate([rows, query.reshape(8, 8 * HD)], axis=0), "y")
    ring = [step_z(memory, memory)]
    ring.append(step_z(*ring[0]))
    both, ring[1] = lax.optimization_barrier((both, ring[1]))
    rows = both[:, :32].reshape(2 * HD, 8 * HD)
    query = both[:, 32:].reshape(512, HD)
    w_a = spread(rows, "x")
    ring.append(step_z(*ring[1]))
    w_a, ring[2] = lax.optimization_barrier((w_a, ring[2]))
    ups, downs = zip(*ring)
    opposite = step_z(ups[2][:128], downs[2][128:])
    own = project((memory, *ups, *downs, *opposite), w_a, swap(w_a))

    own = lax.all_gather(own, "x", axis=0, tiled=True)
    parts = attend(query, own, swap(own))
    parts = lax.all_to_all(parts, "y", 0, 0, tiled=True)
    result = merge(parts)
    return lax.ppermute(result, ALL, query_moves())


def solution(mesh):
    fine = Mesh(mesh.devices.reshape(8, 4, 2, 8), ALL)
    ctx = ("y", "x", "c")
    return jax.shard_map(
        body,
        mesh=fine,
        in_specs=(P(ctx, "z"), P(ctx, "z"), P("z", ctx)),
        out_specs=P("z", ctx),
        check_vma=False,
    )
```

```python
import jax
import jax.numpy as jnp
from jax import lax
from jax.experimental import pallas as pl
from jax.experimental.pallas import tpu as pltpu
from jax.sharding import Mesh, PartitionSpec as P

HD = 128
NT = (((1,), (1,)), ((), ()))
NN = (((1,), (0,)), ((), ()))


def spread(value, axis):
    count = lax.axis_size(axis)
    copies = jnp.broadcast_to(value[None], (count,) + value.shape)
    return lax.all_to_all(copies, axis, 0, 0, tiled=True)


def place(y, x, c, z):
    return ((y * 4 + x) * 2 + c) * 8 + z


def weight_moves():
    moves = []
    for y in range(8):
        for x in range(4):
            for c in range(2):
                shard = y * 8 + x * 2 + c
                kind, head, quarter = shard // 32, shard // 4 % 8, shard % 4
                for z in range(8):
                    moves.append((place(y, x, c, z), place(kind * 4 + quarter, z // 2, z % 2, head)))
    return moves


def exchange_moves():
    return [
        (place(y, x, c, z), place(z, x, c, y)) for y in range(8) for x in range(4) for c in range(2) for z in range(8)
    ]


ALL = ("y", "x", "c", "z")
def shift(count, away):
    return [(i, (i + away) % count) for i in range(count)]


SWAP = [(0, 1), (1, 0)]


def project_kernel(*refs):
    mem, (mem_a, mem_b, w_a, w_b, out_ref, held, sems) = refs[:7], refs[7:]
    core, z = lax.axis_index("c"), lax.axis_index("z")
    copies = [pltpu.make_async_copy(ref, held.at[j], sems.at[j]) for j, ref in enumerate(mem)]
    copies.append(pltpu.make_async_copy(mem_a, held.at[7, pl.ds(0, 128)], sems.at[7]))
    copies.append(pltpu.make_async_copy(mem_b, held.at[7, pl.ds(128, 128)], sems.at[8]))
    for copy in copies:
        copy.start()

    def run(even, odd):
        total = None
        for j, away in enumerate((0, 7, 6, 5, 1, 2, 3, 4)):
            copies[j].wait()
            if j == 7:
                copies[8].wait()
            rows = (even, odd)[away % 2][lax.rem(z + away, 8) // 2]
            part = lax.dot_general(held[j], rows, NT, preferred_element_type=jnp.float32)
            total = part if total is None else total + part
        out_ref[...] = total.astype(out_ref.dtype)

    @pl.when(lax.rem(z, 2) == core)
    def _():
        run(w_a, w_b)

    @pl.when(lax.rem(z, 2) != core)
    def _():
        run(w_b, w_a)


def project(mem, w_a, w_b):
    vmem = pl.BlockSpec(memory_space=pltpu.VMEM)
    return pl.pallas_call(
        project_kernel,
        out_shape=jax.ShapeDtypeStruct((256, 2 * HD), jnp.bfloat16),
        in_specs=[pl.BlockSpec(memory_space=pl.ANY)] * 9 + [vmem] * 2,
        out_specs=vmem,
        scratch_shapes=[pltpu.VMEM((8, 256, 8 * HD), jnp.bfloat16), pltpu.SemaphoreType.DMA((9,))],
        compiler_params=pltpu.CompilerParams(vmem_limit_bytes=50 << 20),
        cost_estimate=pl.CostEstimate(flops=2 * 256 * 256 * 8192, bytes_accessed=8 << 20, transcendentals=0),
    )(*mem, w_a, w_b)


def attend_kernel(q_ref, own, other, out_ref):
    blocks = [(ref, start) for ref in (own, other) for start in range(0, 1024, 256)]
    query = q_ref[...]
    top = total = acc = None
    for ref, start in blocks:
        keys = ref[start : start + 256, :HD]
        values = ref[start : start + 256, HD:]
        scores = lax.dot_general(query, keys, NT, preferred_element_type=jnp.float32) * HD ** (-0.5)
        block_max = jnp.max(scores, axis=1, keepdims=True)
        expo = jnp.exp(scores - block_max)
        block_total = jnp.sum(expo, axis=1, keepdims=True)
        block_out = lax.dot_general(expo.astype(jnp.bfloat16), values, NN, preferred_element_type=jnp.float32)
        if top is None:
            top, total, acc = block_max, block_total, block_out
        else:
            new_top = jnp.maximum(top, block_max)
            keep, add = jnp.exp(top - new_top), jnp.exp(block_max - new_top)
            total = total * keep + block_total * add
            acc = acc * keep + block_out * add
            top = new_top
    tops = jnp.concatenate([top[h * 64 : h * 64 + 64] for h in range(8)], axis=1)
    totals = jnp.concatenate([total[h * 64 : h * 64 + 64] for h in range(8)], axis=1)
    stats = jnp.concatenate([tops, totals], axis=0).T
    for h in range(8):
        out_ref[h, :64, :] = acc[h * 64 : h * 64 + 64]
        out_ref[h, 64:, :] = jnp.broadcast_to(stats[h : h + 1], (8, HD))


def attend(query, own, other):
    return pl.pallas_call(
        attend_kernel,
        out_shape=jax.ShapeDtypeStruct((8, 72, HD), jnp.float32),
        compiler_params=pltpu.CompilerParams(vmem_limit_bytes=16 << 20),
        cost_estimate=pl.CostEstimate(
            flops=4 * 512 * 2048 * HD, bytes_accessed=2 << 20, transcendentals=512 * 2048
        ),
    )(query, own, other)


def merge_kernel(part_ref, out_ref):
    stats = jnp.concatenate([part_ref[j, 64:65, :] for j in range(8)], axis=0).T
    tops, totals = stats[:64], stats[64:]
    top = jnp.max(tops, axis=1, keepdims=True)
    factor = jnp.exp(tops - top)
    denom = jnp.sum(factor * totals, axis=1, keepdims=True)
    numer = factor[:, :1] * part_ref[0, :64, :]
    for j in range(1, 8):
        numer += factor[:, j : j + 1] * part_ref[j, :64, :]
    out_ref[...] = (numer / denom).astype(out_ref.dtype)


def merge(parts):
    return pl.pallas_call(
        merge_kernel,
        out_shape=jax.ShapeDtypeStruct((64, HD), jnp.bfloat16),
    )(parts)


def step_z(ups, downs):
    return lax.ppermute(ups, "z", shift(8, 1)), lax.ppermute(downs, "z", shift(8, -1))


def swap(value):
    return lax.ppermute(value, "c", SWAP)


def body(memory, kv_weight, queries):
    rows = lax.ppermute(kv_weight, ALL, weight_moves())
    ring = [step_z(memory, memory)]
    rows = spread(rows, "y").reshape(2 * HD, 8 * HD)
    ring.append(step_z(*ring[0]))
    rows, ring[1] = lax.optimization_barrier((rows, ring[1]))
    w_a = spread(rows, "x")
    ring.append(step_z(*ring[1]))
    w_a, ring[2], queries = lax.optimization_barrier((w_a, ring[2], queries))
    ups, downs = zip(*ring)
    opposite = step_z(ups[2][:128], downs[2][128:])
    query = spread(queries, "z").reshape(512, HD)
    opposite, query = lax.optimization_barrier((opposite, query))
    own = project((memory, *ups, *downs, *opposite), w_a, swap(w_a))

    own = lax.ppermute(own, ALL, exchange_moves())
    own = lax.all_gather(own, "x", axis=0, tiled=True)
    parts = attend(query, own, swap(own))
    return merge(lax.all_to_all(parts, "z", 0, 0, tiled=True))


def solution(mesh):
    fine = Mesh(mesh.devices.reshape(8, 4, 2, 8), ALL)
    ctx = ("y", "x", "c")
    return jax.shard_map(
        body,
        mesh=fine,
        in_specs=(P(ctx, "z"), P(ctx, "z"), P("z", ctx)),
        out_specs=P("z", ctx),
        check_vma=False,
    )
```

```python
import jax
import jax.numpy as jnp
from jax import lax
from jax.experimental import pallas as pl
from jax.experimental.pallas import tpu as pltpu
from jax.sharding import Mesh, PartitionSpec as P

HD = 128
NT = (((1,), (1,)), ((), ()))
NN = (((1,), (0,)), ((), ()))


def spread(value, axis):
    count = lax.axis_size(axis)
    copies = jnp.broadcast_to(value[None], (count,) + value.shape)
    return lax.all_to_all(copies, axis, 0, 0, tiled=True)


def place(y, x, c, z):
    return ((y * 4 + x) * 2 + c) * 8 + z


def weight_moves():
    moves = []
    for y in range(8):
        for x in range(4):
            for c in range(2):
                shard = y * 8 + x * 2 + c
                kind, head, quarter = shard // 32, shard // 4 % 8, shard % 4
                for z in range(8):
                    moves.append((place(y, x, c, z), place(kind * 4 + quarter, z // 2, z % 2, head)))
    return moves


def query_moves():
    return [
        (place(y, x, c, z), place(z, x, c, y)) for y in range(8) for x in range(4) for c in range(2) for z in range(8)
    ]


ALL = ("y", "x", "c", "z")
def shift(count, away):
    return [(i, (i + away) % count) for i in range(count)]


SWAP = [(0, 1), (1, 0)]


def project_kernel(mem_ref, *refs):
    w_refs, (out_ref, held, sems) = refs[:10], refs[10:]
    x, core = lax.axis_index("x"), lax.axis_index("c")
    order = [(swapped, away) for away in (0, 3, 1, 2) for swapped in (0, 1)]
    copies = []
    for j, (swapped, away) in enumerate(order):
        half = core if swapped == 0 else 1 - core
        share = lax.rem(x + away, 4) * 2 + half
        copies.append(pltpu.make_async_copy(mem_ref.at[share], held.at[j], sems.at[j]))
        copies[j].start()
    keys = values = None
    for j, (swapped, away) in enumerate(order):
        own, left, right, opp_k, opp_v = w_refs[5 * swapped : 5 * swapped + 5]
        if away == 2:
            k_rows, v_rows = opp_k[...], opp_v[...]
        else:
            ref = {0: own, 3: left, 1: right}[away]
            k_rows, v_rows = ref[:HD], ref[HD:]
        copies[j].wait()
        k_part = lax.dot_general(held[j], k_rows, NT, preferred_element_type=jnp.float32)
        v_part = lax.dot_general(held[j], v_rows, NT, preferred_element_type=jnp.float32)
        keys = k_part if keys is None else keys + k_part
        values = v_part if values is None else values + v_part
    out_ref[:, :HD] = keys.astype(out_ref.dtype)
    out_ref[:, HD:] = values.astype(out_ref.dtype)


def project(mem_all, w_pieces):
    vmem = pl.BlockSpec(memory_space=pltpu.VMEM)
    return pl.pallas_call(
        project_kernel,
        out_shape=jax.ShapeDtypeStruct((256, 2 * HD), jnp.bfloat16),
        in_specs=[pl.BlockSpec(memory_space=pl.ANY)] + [vmem] * 10,
        out_specs=vmem,
        scratch_shapes=[pltpu.VMEM(mem_all.shape, jnp.bfloat16), pltpu.SemaphoreType.DMA((8,))],
        compiler_params=pltpu.CompilerParams(vmem_limit_bytes=50 << 20),
        cost_estimate=pl.CostEstimate(flops=2 * 256 * 256 * 8192, bytes_accessed=8 << 20, transcendentals=0),
    )(mem_all, *w_pieces)


def attend_kernel(q_ref, own, other, out_ref):
    blocks = [(ref, start) for ref in (own, other) for start in range(0, 1024, 256)]
    query = q_ref[...]
    top = total = acc = None
    for ref, start in blocks:
        keys = ref[start : start + 256, :HD]
        values = ref[start : start + 256, HD:]
        scores = lax.dot_general(query, keys, NT, preferred_element_type=jnp.float32) * HD ** (-0.5)
        block_max = jnp.max(scores, axis=1, keepdims=True)
        expo = jnp.exp(scores - block_max)
        block_total = jnp.sum(expo, axis=1, keepdims=True)
        block_out = lax.dot_general(expo.astype(jnp.bfloat16), values, NN, preferred_element_type=jnp.float32)
        if top is None:
            top, total, acc = block_max, block_total, block_out
        else:
            new_top = jnp.maximum(top, block_max)
            keep, add = jnp.exp(top - new_top), jnp.exp(block_max - new_top)
            total = total * keep + block_total * add
            acc = acc * keep + block_out * add
            top = new_top
    tops = jnp.concatenate([top[h * 64 : h * 64 + 64] for h in range(8)], axis=1)
    totals = jnp.concatenate([total[h * 64 : h * 64 + 64] for h in range(8)], axis=1)
    stats = jnp.concatenate([tops, totals], axis=0).T
    for h in range(8):
        out_ref[h, :64, :] = acc[h * 64 : h * 64 + 64]
        out_ref[h, 64:, :] = jnp.broadcast_to(stats[h : h + 1], (8, HD))


def attend(query, own, other):
    return pl.pallas_call(
        attend_kernel,
        out_shape=jax.ShapeDtypeStruct((8, 72, HD), jnp.float32),
        compiler_params=pltpu.CompilerParams(vmem_limit_bytes=24 << 20),
        cost_estimate=pl.CostEstimate(
            flops=4 * 512 * 2048 * HD, bytes_accessed=2 << 20, transcendentals=512 * 2048
        ),
    )(query, own, other)


def merge_kernel(part_ref, out_ref):
    stats = jnp.concatenate([part_ref[j, 64:65, :] for j in range(8)], axis=0).T
    tops, totals = stats[:64], stats[64:]
    top = jnp.max(tops, axis=1, keepdims=True)
    factor = jnp.exp(tops - top)
    denom = jnp.sum(factor * totals, axis=1, keepdims=True)
    numer = factor[:, :1] * part_ref[0, :64, :]
    for j in range(1, 8):
        numer += factor[:, j : j + 1] * part_ref[j, :64, :]
    out_ref[...] = (numer / denom).astype(out_ref.dtype)


def merge(parts):
    return pl.pallas_call(
        merge_kernel,
        out_shape=jax.ShapeDtypeStruct((64, HD), jnp.bfloat16),
    )(parts)


def ring(value):
    half = value.shape[0] // 2
    left = lax.ppermute(value, "x", shift(4, 1))
    right = lax.ppermute(value, "x", shift(4, -1))
    opp_a = lax.ppermute(left[:half], "x", shift(4, 1))
    opp_b = lax.ppermute(right[half:], "x", shift(4, -1))
    return value, left, right, opp_a, opp_b


def swap(value):
    return lax.ppermute(value, "c", SWAP)


def body(memory, kv_weight, queries):
    mem_all = lax.all_gather(memory, "z", axis=0)
    rows = lax.ppermute(kv_weight, ALL, weight_moves())
    query = lax.ppermute(queries, ALL, query_moves())
    both = spread(jnp.concatenate([rows, query.reshape(8, 8 * HD)], axis=0), "y")
    rows = both[:, :32].reshape(2 * HD, 8 * HD)
    query = both[:, 32:].reshape(512, HD)
    w_pieces = ring(rows)
    own = project(mem_all, (*w_pieces, *map(swap, w_pieces)))

    own = lax.all_gather(own, "x", axis=0, tiled=True)
    parts = attend(query, own, swap(own))
    parts = lax.all_to_all(parts, "y", 0, 0, tiled=True)
    result = merge(parts)
    return lax.ppermute(result, ALL, query_moves())


def solution(mesh):
    fine = Mesh(mesh.devices.reshape(8, 4, 2, 8), ALL)
    ctx = ("y", "x", "c")
    return jax.shard_map(
        body,
        mesh=fine,
        in_specs=(P(ctx, "z"), P(ctx, "z"), P("z", ctx)),
        out_specs=P("z", ctx),
        check_vma=False,
    )
```

```python
import jax
import jax.numpy as jnp
from jax import lax
from jax.experimental import pallas as pl
from jax.experimental.pallas import tpu as pltpu
from jax.sharding import Mesh, PartitionSpec as P

HD = 128
NT = (((1,), (1,)), ((), ()))
NN = (((1,), (0,)), ((), ()))


def spread(value, axis):
    count = lax.axis_size(axis)
    copies = jnp.broadcast_to(value[None], (count,) + value.shape)
    return lax.all_to_all(copies, axis, 0, 0, tiled=True)


def place(y, x, c, z):
    return ((y * 4 + x) * 2 + c) * 8 + z


def weight_moves():
    moves = []
    for y in range(8):
        for x in range(4):
            for c in range(2):
                shard = y * 8 + x * 2 + c
                kind, head, quarter = shard // 32, shard // 4 % 8, shard % 4
                for z in range(8):
                    target = place(kind * 4 + quarter, z // 2, z % 2, (head + 4) % 8)
                    moves.append((place(y, x, c, z), target))
    return moves


def query_moves():
    return [
        (place(y, x, c, z), place(z, x, c, (y + 4) % 8))
        for y in range(8)
        for x in range(4)
        for c in range(2)
        for z in range(8)
    ]


ALL = ("y", "x", "c", "z")
def shift(count, away):
    return [(i, (i + away) % count) for i in range(count)]


SWAP = [(0, 1), (1, 0)]


def project_kernel(mem_ref, *refs):
    w_refs, (out_ref, mem_held, w_held, mem_sems, w_sems) = refs[:10], refs[10:]
    x, core = lax.axis_index("x"), lax.axis_index("c")
    order = [(swapped, away) for away in (0, 3, 1, 2) for swapped in (0, 1)]
    copies = []
    for j, (swapped, away) in enumerate(order):
        half = core if swapped == 0 else 1 - core
        share = lax.rem(x + away, 4) * 2 + half
        own, left, right, opp_k, opp_v = w_refs[5 * swapped : 5 * swapped + 5]
        if away == 2:
            pairs = [(opp_k, w_held.at[j, pl.ds(0, HD)]), (opp_v, w_held.at[j, pl.ds(HD, HD)])]
        else:
            pairs = [({0: own, 3: left, 1: right}[away], w_held.at[j])]
        moves = [pltpu.make_async_copy(mem_ref.at[share], mem_held.at[j], mem_sems.at[j])]
        moves += [pltpu.make_async_copy(src, dst, w_sems.at[j, i]) for i, (src, dst) in enumerate(pairs)]
        for move in moves:
            move.start()
        copies.append(moves)
    total = None
    for j, moves in enumerate(copies):
        for move in moves:
            move.wait()
        part = lax.dot_general(mem_held[j], w_held[j], NT, preferred_element_type=jnp.float32)
        total = part if total is None else total + part
    out_ref[...] = total.astype(out_ref.dtype)


def project(mem_all, w_pieces):
    return pl.pallas_call(
        project_kernel,
        out_shape=jax.ShapeDtypeStruct((256, 2 * HD), jnp.bfloat16),
        in_specs=[pl.BlockSpec(memory_space=pl.ANY)] * 11,
        out_specs=pl.BlockSpec(memory_space=pltpu.VMEM),
        scratch_shapes=[
            pltpu.VMEM(mem_all.shape, jnp.bfloat16),
            pltpu.VMEM(mem_all.shape, jnp.bfloat16),
            pltpu.SemaphoreType.DMA((8,)),
            pltpu.SemaphoreType.DMA((8, 2)),
        ],
        compiler_params=pltpu.CompilerParams(vmem_limit_bytes=52 << 20),
        cost_estimate=pl.CostEstimate(flops=2 * 256 * 256 * 8192, bytes_accessed=8 << 20, transcendentals=0),
    )(mem_all, *w_pieces)


def attend_kernel(q_ref, own, other, out_ref):
    blocks = [(ref, start) for ref in (own, other) for start in range(0, 1024, 256)]
    query = q_ref[...]
    top = total = acc = None
    for ref, start in blocks:
        keys = ref[start : start + 256, :HD]
        values = ref[start : start + 256, HD:]
        scores = lax.dot_general(query, keys, NT, preferred_element_type=jnp.float32) * HD ** (-0.5)
        block_max = jnp.max(scores, axis=1, keepdims=True)
        expo = jnp.exp(scores - block_max)
        block_total = jnp.sum(expo, axis=1, keepdims=True)
        block_out = lax.dot_general(expo.astype(jnp.bfloat16), values, NN, preferred_element_type=jnp.float32)
        if top is None:
            top, total, acc = block_max, block_total, block_out
        else:
            new_top = jnp.maximum(top, block_max)
            keep, add = jnp.exp(top - new_top), jnp.exp(block_max - new_top)
            total = total * keep + block_total * add
            acc = acc * keep + block_out * add
            top = new_top
    tops = jnp.concatenate([top[h * 64 : h * 64 + 64] for h in range(8)], axis=1)
    totals = jnp.concatenate([total[h * 64 : h * 64 + 64] for h in range(8)], axis=1)
    stats = jnp.concatenate([tops, totals], axis=0).T
    for h in range(8):
        out_ref[h, :64, :] = acc[h * 64 : h * 64 + 64]
        out_ref[h, 64:, :] = jnp.broadcast_to(stats[h : h + 1], (8, HD))


def attend(query, own, other):
    return pl.pallas_call(
        attend_kernel,
        out_shape=jax.ShapeDtypeStruct((8, 72, HD), jnp.float32),
        compiler_params=pltpu.CompilerParams(vmem_limit_bytes=24 << 20),
        cost_estimate=pl.CostEstimate(
            flops=4 * 512 * 2048 * HD, bytes_accessed=2 << 20, transcendentals=512 * 2048
        ),
    )(query, own, other)


def merge_kernel(part_ref, out_ref):
    stats = jnp.concatenate([part_ref[j, 64:65, :] for j in range(8)], axis=0).T
    tops, totals = stats[:64], stats[64:]
    top = jnp.max(tops, axis=1, keepdims=True)
    factor = jnp.exp(tops - top)
    denom = jnp.sum(factor * totals, axis=1, keepdims=True)
    numer = factor[:, :1] * part_ref[0, :64, :]
    for j in range(1, 8):
        numer += factor[:, j : j + 1] * part_ref[j, :64, :]
    out_ref[...] = (numer / denom).astype(out_ref.dtype)


def merge(parts):
    return pl.pallas_call(
        merge_kernel,
        out_shape=jax.ShapeDtypeStruct((64, HD), jnp.bfloat16),
    )(parts)


def ring(value):
    half = value.shape[0] // 2
    left = lax.ppermute(value, "x", shift(4, 1))
    right = lax.ppermute(value, "x", shift(4, -1))
    opp_a = lax.ppermute(left[:half], "x", shift(4, 1))
    opp_b = lax.ppermute(right[half:], "x", shift(4, -1))
    return value, left, right, opp_a, opp_b


def swap(value):
    return lax.ppermute(value, "c", SWAP)


def body(memory, kv_weight, queries):
    mem_all = lax.all_gather(memory, "z", axis=0)
    rows = lax.ppermute(kv_weight, ALL, weight_moves())
    query = lax.ppermute(queries, ALL, query_moves())
    both = lax.all_gather(jnp.concatenate([rows, query.reshape(8, 8 * HD)], axis=0), "y", axis=0)
    rows = both[:, :32].reshape(2 * HD, 8 * HD)
    query = both[:, 32:].reshape(512, HD)
    w_pieces = ring(rows)
    own = project(mem_all, (*w_pieces, *map(swap, w_pieces)))

    own = lax.all_gather(own, "x", axis=0, tiled=True)
    parts = attend(query, own, swap(own))
    parts = lax.all_to_all(parts, "y", 0, 0, tiled=True)
    result = merge(parts)
    return lax.ppermute(result, ALL, [(b, a) for a, b in query_moves()])


def solution(mesh):
    fine = Mesh(mesh.devices.reshape(8, 4, 2, 8), ALL)
    ctx = ("y", "x", "c")
    return jax.shard_map(
        body,
        mesh=fine,
        in_specs=(P(ctx, "z"), P(ctx, "z"), P("z", ctx)),
        out_specs=P("z", ctx),
        check_vma=False,
    )
```

```python
import jax
import jax.numpy as jnp
from jax import lax
from jax.experimental import pallas as pl
from jax.experimental.pallas import tpu as pltpu
from jax.sharding import Mesh, PartitionSpec as P

HD = 128
NT = (((1,), (1,)), ((), ()))
NN = (((1,), (0,)), ((), ()))


def spread(value, axis):
    count = lax.axis_size(axis)
    copies = jnp.broadcast_to(value[None], (count,) + value.shape)
    return lax.all_to_all(copies, axis, 0, 0, tiled=True)


def place(y, x, c, z):
    return ((y * 4 + x) * 2 + c) * 8 + z


def weight_moves():
    moves = []
    for y in range(8):
        for x in range(4):
            for c in range(2):
                shard = y * 8 + x * 2 + c
                kind, head, quarter = shard // 32, shard // 4 % 8, shard % 4
                for z in range(8):
                    target = place(kind * 4 + quarter, z // 2, z % 2, (head + 4) % 8)
                    moves.append((place(y, x, c, z), target))
    return moves


def query_moves():
    return [
        (place(y, x, c, z), place(z, x, c, (y + 4) % 8))
        for y in range(8)
        for x in range(4)
        for c in range(2)
        for z in range(8)
    ]


ALL = ("y", "x", "c", "z")
def shift(count, away):
    return [(i, (i + away) % count) for i in range(count)]


SWAP = [(0, 1), (1, 0)]


def project_kernel(mem_ref, *refs):
    w_refs, (out_ref, held, sems) = refs[:8], refs[8:]
    x, core = lax.axis_index("x"), lax.axis_index("c")
    near, far, across = lax.rem(x + 3 + 2 * core, 4), lax.rem(x + 1 + 2 * core, 4), lax.rem(x + 2, 4)
    shares = [
        2 * x + core,
        2 * x + 1 - core,
        2 * near + core,
        2 * near + 1 - core,
        2 * across + core,
        2 * far + 1 - core,
        2 * far + core,
        2 * across + 1 - core,
    ]
    copies = [pltpu.make_async_copy(mem_ref.at[share], held.at[j], sems.at[j]) for j, share in enumerate(shares)]
    for copy in copies:
        copy.start()
    total = None
    for j, w_ref in enumerate(w_refs):
        copies[j].wait()
        part = lax.dot_general(held[j], w_ref[...], NT, preferred_element_type=jnp.float32)
        total = part if total is None else total + part
    out_ref[...] = total.astype(out_ref.dtype)


def project(mem_all, w_pieces):
    vmem = pl.BlockSpec(memory_space=pltpu.VMEM)
    return pl.pallas_call(
        project_kernel,
        out_shape=jax.ShapeDtypeStruct((256, 2 * HD), jnp.bfloat16),
        in_specs=[pl.BlockSpec(memory_space=pl.ANY)] + [vmem] * 8,
        out_specs=vmem,
        scratch_shapes=[pltpu.VMEM(mem_all.shape, jnp.bfloat16), pltpu.SemaphoreType.DMA((8,))],
        compiler_params=pltpu.CompilerParams(vmem_limit_bytes=50 << 20),
        cost_estimate=pl.CostEstimate(flops=2 * 256 * 256 * 8192, bytes_accessed=8 << 20, transcendentals=0),
    )(mem_all, *w_pieces)


def attend_kernel(q_ref, own, other, out_ref):
    blocks = [(ref, start) for ref in (own, other) for start in range(0, 1024, 256)]
    query = q_ref[...]
    top = total = acc = None
    for ref, start in blocks:
        keys = ref[start : start + 256, :HD]
        values = ref[start : start + 256, HD:]
        scores = lax.dot_general(query, keys, NT, preferred_element_type=jnp.float32) * HD ** (-0.5)
        block_max = jnp.max(scores, axis=1, keepdims=True)
        expo = jnp.exp(scores - block_max)
        block_total = jnp.sum(expo, axis=1, keepdims=True)
        block_out = lax.dot_general(expo.astype(jnp.bfloat16), values, NN, preferred_element_type=jnp.float32)
        if top is None:
            top, total, acc = block_max, block_total, block_out
        else:
            new_top = jnp.maximum(top, block_max)
            keep, add = jnp.exp(top - new_top), jnp.exp(block_max - new_top)
            total = total * keep + block_total * add
            acc = acc * keep + block_out * add
            top = new_top
    tops = jnp.concatenate([top[h * 64 : h * 64 + 64] for h in range(8)], axis=1)
    totals = jnp.concatenate([total[h * 64 : h * 64 + 64] for h in range(8)], axis=1)
    stats = jnp.concatenate([tops, totals], axis=0).T
    for h in range(8):
        out_ref[h, :64, :] = acc[h * 64 : h * 64 + 64]
        out_ref[h, 64:, :] = jnp.broadcast_to(stats[h : h + 1], (8, HD))


def attend(query, own, other):
    return pl.pallas_call(
        attend_kernel,
        out_shape=jax.ShapeDtypeStruct((8, 72, HD), jnp.float32),
        compiler_params=pltpu.CompilerParams(vmem_limit_bytes=24 << 20),
        cost_estimate=pl.CostEstimate(
            flops=4 * 512 * 2048 * HD, bytes_accessed=2 << 20, transcendentals=512 * 2048
        ),
    )(query, own, other)


def merge_kernel(part_ref, out_ref):
    stats = jnp.concatenate([part_ref[j, 64:65, :] for j in range(8)], axis=0).T
    tops, totals = stats[:64], stats[64:]
    top = jnp.max(tops, axis=1, keepdims=True)
    factor = jnp.exp(tops - top)
    denom = jnp.sum(factor * totals, axis=1, keepdims=True)
    numer = factor[:, :1] * part_ref[0, :64, :]
    for j in range(1, 8):
        numer += factor[:, j : j + 1] * part_ref[j, :64, :]
    out_ref[...] = (numer / denom).astype(out_ref.dtype)


def merge(parts):
    return pl.pallas_call(
        merge_kernel,
        out_shape=jax.ShapeDtypeStruct((64, HD), jnp.bfloat16),
    )(parts)


def turn(value):
    return lax.ppermute(value, ("x", "c"), [(2 * i + c, (i + 1 + 2 * c) % 4 * 2 + c) for i in range(4) for c in range(2)])


def pieces_over_x(own):
    first = turn(own)
    own_swapped = swap(own)
    across = turn(first)
    second = turn(own_swapped)
    return own, own_swapped, first, second, across, swap(first), swap(second), swap(across)


def swap(value):
    return lax.ppermute(value, "c", SWAP)


def body(memory, kv_weight, queries):
    mem_all = lax.all_gather(memory, "z", axis=0)
    rows = lax.ppermute(kv_weight, ALL, weight_moves())
    query = lax.ppermute(queries, ALL, query_moves())
    both = lax.all_gather(jnp.concatenate([rows, query.reshape(8, 8 * HD)], axis=0), "y", axis=0)
    rows = both[:, :32].reshape(2 * HD, 8 * HD)
    query = both[:, 32:].reshape(512, HD)
    w_pieces = pieces_over_x(rows)
    own = project(mem_all, w_pieces)

    own = lax.all_gather(own, "x", axis=0, tiled=True)
    parts = attend(query, own, swap(own))
    parts = lax.all_to_all(parts, "y", 0, 0, tiled=True)
    result = merge(parts)
    return lax.ppermute(result, ALL, [(b, a) for a, b in query_moves()])


def solution(mesh):
    fine = Mesh(mesh.devices.reshape(8, 4, 2, 8), ALL)
    ctx = ("y", "x", "c")
    return jax.shard_map(
        body,
        mesh=fine,
        in_specs=(P(ctx, "z"), P(ctx, "z"), P("z", ctx)),
        out_specs=P("z", ctx),
        check_vma=False,
    )
```

```python
import jax
import jax.numpy as jnp
from jax import lax
from jax.experimental import pallas as pl
from jax.experimental.pallas import tpu as pltpu
from jax.sharding import Mesh, PartitionSpec as P

HD = 128
NT = (((1,), (1,)), ((), ()))
NN = (((1,), (0,)), ((), ()))


def spread(value, axis):
    count = lax.axis_size(axis)
    copies = jnp.broadcast_to(value[None], (count,) + value.shape)
    return lax.all_to_all(copies, axis, 0, 0, tiled=True)


def place(y, x, c, z):
    return ((y * 4 + x) * 2 + c) * 8 + z


def weight_moves():
    moves = []
    for y in range(8):
        for x in range(4):
            for c in range(2):
                shard = y * 8 + x * 2 + c
                kind, head, quarter = shard // 32, shard // 4 % 8, shard % 4
                for z in range(8):
                    target = place(kind * 4 + quarter, z // 2, z % 2, (head + 4) % 8)
                    moves.append((place(y, x, c, z), target))
    return moves


def query_moves():
    return [
        (place(y, x, c, z), place(z, x, c, (y + 4) % 8))
        for y in range(8)
        for x in range(4)
        for c in range(2)
        for z in range(8)
    ]


ALL = ("y", "x", "c", "z")
def shift(count, away):
    return [(i, (i + away) % count) for i in range(count)]


SWAP = [(0, 1), (1, 0)]


def project_kernel(mem_ref, *refs):
    w_refs, (out_ref, held, sems) = refs[:10], refs[10:]
    x, core = lax.axis_index("x"), lax.axis_index("c")
    order = [(swapped, away) for away in (0, 3, 1, 2) for swapped in (0, 1)]
    copies = []
    for j, (swapped, away) in enumerate(order):
        half = core if swapped == 0 else 1 - core
        share = lax.rem(x + away, 4) * 2 + half
        copies.append(pltpu.make_async_copy(mem_ref.at[share], held.at[j], sems.at[j]))
        copies[j].start()
    total = None
    for j, (swapped, away) in enumerate(order):
        own, left, right, opp_k, opp_v = w_refs[5 * swapped : 5 * swapped + 5]
        if away == 2:
            w_rows = jnp.concatenate([opp_k[...], opp_v[...]], axis=0)
        else:
            w_rows = {0: own, 3: left, 1: right}[away][...]
        copies[j].wait()
        part = lax.dot_general(held[j], w_rows, NT, preferred_element_type=jnp.float32)
        total = part if total is None else total + part
    out_ref[...] = total.astype(out_ref.dtype)


def project(mem_all, w_pieces):
    vmem = pl.BlockSpec(memory_space=pltpu.VMEM)
    return pl.pallas_call(
        project_kernel,
        out_shape=jax.ShapeDtypeStruct((256, 2 * HD), jnp.bfloat16),
        in_specs=[pl.BlockSpec(memory_space=pl.ANY)] + [vmem] * 10,
        out_specs=vmem,
        scratch_shapes=[pltpu.VMEM(mem_all.shape, jnp.bfloat16), pltpu.SemaphoreType.DMA((8,))],
        compiler_params=pltpu.CompilerParams(vmem_limit_bytes=50 << 20),
        cost_estimate=pl.CostEstimate(flops=2 * 256 * 256 * 8192, bytes_accessed=8 << 20, transcendentals=0),
    )(mem_all, *w_pieces)


def attend_kernel(q_ref, own, other, out_ref):
    blocks = [(ref, start) for ref in (own, other) for start in range(0, 1024, 256)]
    query = q_ref[...]
    top = total = acc = None
    for ref, start in blocks:
        keys = ref[start : start + 256, :HD]
        values = ref[start : start + 256, HD:]
        scores = lax.dot_general(query, keys, NT, preferred_element_type=jnp.float32) * HD ** (-0.5)
        block_max = jnp.max(scores, axis=1, keepdims=True)
        expo = jnp.exp(scores - block_max)
        block_total = jnp.sum(expo, axis=1, keepdims=True)
        block_out = lax.dot_general(expo.astype(jnp.bfloat16), values, NN, preferred_element_type=jnp.float32)
        if top is None:
            top, total, acc = block_max, block_total, block_out
        else:
            new_top = jnp.maximum(top, block_max)
            keep, add = jnp.exp(top - new_top), jnp.exp(block_max - new_top)
            total = total * keep + block_total * add
            acc = acc * keep + block_out * add
            top = new_top
    tops = jnp.concatenate([top[h * 64 : h * 64 + 64] for h in range(8)], axis=1)
    totals = jnp.concatenate([total[h * 64 : h * 64 + 64] for h in range(8)], axis=1)
    stats = jnp.concatenate([tops, totals], axis=0).T
    for h in range(8):
        out_ref[h, :64, :] = acc[h * 64 : h * 64 + 64]
        out_ref[h, 64:, :] = jnp.broadcast_to(stats[h : h + 1], (8, HD))


def attend(query, own, other):
    return pl.pallas_call(
        attend_kernel,
        out_shape=jax.ShapeDtypeStruct((8, 72, HD), jnp.float32),
        compiler_params=pltpu.CompilerParams(vmem_limit_bytes=24 << 20),
        cost_estimate=pl.CostEstimate(
            flops=4 * 512 * 2048 * HD, bytes_accessed=2 << 20, transcendentals=512 * 2048
        ),
    )(query, own, other)


def merge_kernel(part_ref, out_ref):
    stats = jnp.concatenate([part_ref[j, 64:65, :] for j in range(8)], axis=0).T
    tops, totals = stats[:64], stats[64:]
    top = jnp.max(tops, axis=1, keepdims=True)
    factor = jnp.exp(tops - top)
    denom = jnp.sum(factor * totals, axis=1, keepdims=True)
    numer = factor[:, :1] * part_ref[0, :64, :]
    for j in range(1, 8):
        numer += factor[:, j : j + 1] * part_ref[j, :64, :]
    out_ref[...] = (numer / denom).astype(out_ref.dtype)


def merge(parts):
    return pl.pallas_call(
        merge_kernel,
        out_shape=jax.ShapeDtypeStruct((64, HD), jnp.bfloat16),
    )(parts)


def ring(value):
    half = value.shape[0] // 2
    left = lax.ppermute(value, "x", shift(4, 1))
    right = lax.ppermute(value, "x", shift(4, -1))
    opp_a = lax.ppermute(left[:half], "x", shift(4, 1))
    opp_b = lax.ppermute(right[half:], "x", shift(4, -1))
    return value, left, right, opp_a, opp_b


def swap(value):
    return lax.ppermute(value, "c", SWAP)


def body(memory, kv_weight, queries):
    mem_all = lax.all_gather(memory, "z", axis=0)
    rows = lax.ppermute(kv_weight, ALL, weight_moves())
    query = lax.ppermute(queries, ALL, query_moves())
    both = spread(jnp.concatenate([rows, query.reshape(8, 8 * HD)], axis=0), "y")
    rows = both[:, :32].reshape(2 * HD, 8 * HD)
    query = both[:, 32:].reshape(512, HD)
    w_pieces = ring(rows)
    own = project(mem_all, (*w_pieces, *map(swap, w_pieces)))

    own = lax.all_gather(own, "x", axis=0, tiled=True)
    parts = attend(query, own, swap(own))
    parts = lax.all_to_all(parts, "y", 0, 0, tiled=True)
    result = merge(parts)
    return lax.ppermute(result, ALL, [(b, a) for a, b in query_moves()])


def solution(mesh):
    fine = Mesh(mesh.devices.reshape(8, 4, 2, 8), ALL)
    ctx = ("y", "x", "c")
    return jax.shard_map(
        body,
        mesh=fine,
        in_specs=(P(ctx, "z"), P(ctx, "z"), P("z", ctx)),
        out_specs=P("z", ctx),
        check_vma=False,
    )
```

```python
import jax
import jax.numpy as jnp
from jax import lax
from jax.experimental import pallas as pl
from jax.experimental.pallas import tpu as pltpu
from jax.sharding import Mesh, PartitionSpec as P

HD = 128
NT = (((1,), (1,)), ((), ()))
NN = (((1,), (0,)), ((), ()))


def spread(value, axis):
    count = lax.axis_size(axis)
    copies = jnp.broadcast_to(value[None], (count,) + value.shape)
    return lax.all_to_all(copies, axis, 0, 0, tiled=True)


def place(y, x, c, z):
    return ((y * 4 + x) * 2 + c) * 8 + z


def weight_moves():
    moves = []
    for y in range(8):
        for x in range(4):
            for c in range(2):
                shard = y * 8 + x * 2 + c
                kind, head, quarter = shard // 32, shard // 4 % 8, shard % 4
                for z in range(8):
                    target = place(kind * 4 + quarter, z // 2, z % 2, (head + 4) % 8)
                    moves.append((place(y, x, c, z), target))
    return moves


def query_moves():
    return [
        (place(y, x, c, z), place(z, x, c, (y + 4) % 8))
        for y in range(8)
        for x in range(4)
        for c in range(2)
        for z in range(8)
    ]


ALL = ("y", "x", "c", "z")
def shift(count, away):
    return [(i, (i + away) % count) for i in range(count)]


SWAP = [(0, 1), (1, 0)]


def project_kernel(mem_ref, *refs):
    w_refs, (out_ref, held, sems) = refs[:10], refs[10:]
    x, core = lax.axis_index("x"), lax.axis_index("c")
    order = [(swapped, away) for away in (0, 3, 1, 2) for swapped in (0, 1)]
    copies = []
    for j, (swapped, away) in enumerate(order):
        half = core if swapped == 0 else 1 - core
        share = lax.rem(x + away, 4) * 2 + half
        for i in range(4):
            part = pl.ds(64 * i, 64)
            copies.append(pltpu.make_async_copy(mem_ref.at[share, part], held.at[j, part], sems.at[j, i]))
            copies[-1].start()
    total = None
    for j, (swapped, away) in enumerate(order):
        own, left, right, opp_k, opp_v = w_refs[5 * swapped : 5 * swapped + 5]
        if away == 2:
            w_rows = jnp.concatenate([opp_k[...], opp_v[...]], axis=0)
        else:
            w_rows = {0: own, 3: left, 1: right}[away][...]
        for copy in copies[4 * j : 4 * j + 4]:
            copy.wait()
        part = lax.dot_general(held[j], w_rows, NT, preferred_element_type=jnp.float32)
        total = part if total is None else total + part
    out_ref[...] = total.astype(out_ref.dtype)


def project(mem_all, w_pieces):
    vmem = pl.BlockSpec(memory_space=pltpu.VMEM)
    return pl.pallas_call(
        project_kernel,
        out_shape=jax.ShapeDtypeStruct((256, 2 * HD), jnp.bfloat16),
        in_specs=[pl.BlockSpec(memory_space=pl.ANY)] + [vmem] * 10,
        out_specs=vmem,
        scratch_shapes=[pltpu.VMEM(mem_all.shape, jnp.bfloat16), pltpu.SemaphoreType.DMA((8, 4))],
        compiler_params=pltpu.CompilerParams(vmem_limit_bytes=46 << 20),
        cost_estimate=pl.CostEstimate(flops=2 * 256 * 256 * 8192, bytes_accessed=8 << 20, transcendentals=0),
    )(mem_all, *w_pieces)


def attend_kernel(q_ref, own, other, out_ref):
    blocks = [(ref, start) for ref in (own, other) for start in range(0, 1024, 256)]
    query = q_ref[...]
    top = total = acc = None
    for ref, start in blocks:
        keys = ref[start : start + 256, :HD]
        values = ref[start : start + 256, HD:]
        scores = lax.dot_general(query, keys, NT, preferred_element_type=jnp.float32) * HD ** (-0.5)
        block_max = jnp.max(scores, axis=1, keepdims=True)
        expo = jnp.exp(scores - block_max)
        block_total = jnp.sum(expo, axis=1, keepdims=True)
        block_out = lax.dot_general(expo.astype(jnp.bfloat16), values, NN, preferred_element_type=jnp.float32)
        if top is None:
            top, total, acc = block_max, block_total, block_out
        else:
            new_top = jnp.maximum(top, block_max)
            keep, add = jnp.exp(top - new_top), jnp.exp(block_max - new_top)
            total = total * keep + block_total * add
            acc = acc * keep + block_out * add
            top = new_top
    tops = jnp.concatenate([top[h * 64 : h * 64 + 64] for h in range(8)], axis=1)
    totals = jnp.concatenate([total[h * 64 : h * 64 + 64] for h in range(8)], axis=1)
    stats = jnp.concatenate([tops, totals], axis=0).T
    for h in range(8):
        out_ref[h, :64, :] = acc[h * 64 : h * 64 + 64]
        out_ref[h, 64:, :] = jnp.broadcast_to(stats[h : h + 1], (8, HD))


def attend(query, own, other):
    return pl.pallas_call(
        attend_kernel,
        out_shape=jax.ShapeDtypeStruct((8, 72, HD), jnp.float32),
        compiler_params=pltpu.CompilerParams(vmem_limit_bytes=24 << 20),
        cost_estimate=pl.CostEstimate(
            flops=4 * 512 * 2048 * HD, bytes_accessed=2 << 20, transcendentals=512 * 2048
        ),
    )(query, own, other)


def merge_kernel(part_ref, out_ref):
    stats = jnp.concatenate([part_ref[j, 64:65, :] for j in range(8)], axis=0).T
    tops, totals = stats[:64], stats[64:]
    top = jnp.max(tops, axis=1, keepdims=True)
    factor = jnp.exp(tops - top)
    denom = jnp.sum(factor * totals, axis=1, keepdims=True)
    numer = factor[:, :1] * part_ref[0, :64, :]
    for j in range(1, 8):
        numer += factor[:, j : j + 1] * part_ref[j, :64, :]
    out_ref[...] = (numer / denom).astype(out_ref.dtype)


def merge(parts):
    return pl.pallas_call(
        merge_kernel,
        out_shape=jax.ShapeDtypeStruct((64, HD), jnp.bfloat16),
    )(parts)


def ring(value):
    half = value.shape[0] // 2
    left = lax.ppermute(value, "x", shift(4, 1))
    right = lax.ppermute(value, "x", shift(4, -1))
    opp_a = lax.ppermute(left[:half], "x", shift(4, 1))
    opp_b = lax.ppermute(right[half:], "x", shift(4, -1))
    return value, left, right, opp_a, opp_b


def swap(value):
    return lax.ppermute(value, "c", SWAP)


def body(memory, kv_weight, queries):
    mem_all = lax.all_gather(memory, "z", axis=0)
    rows = lax.ppermute(kv_weight, ALL, weight_moves())
    query = lax.ppermute(queries, ALL, query_moves())
    both = spread(jnp.concatenate([rows, query.reshape(8, 8 * HD)], axis=0), "y")
    rows = both[:, :32].reshape(2 * HD, 8 * HD)
    query = both[:, 32:].reshape(512, HD)
    *w_pieces, opp_k, opp_v = ring(rows)
    opp_k, opp_v, mem_all = lax.optimization_barrier((opp_k, opp_v, mem_all))
    w_pieces += [opp_k, opp_v]
    own = project(mem_all, (*w_pieces, *map(swap, w_pieces)))

    own = lax.all_gather(own, "x", axis=0, tiled=True)
    parts = attend(query, own, swap(own))
    parts = lax.all_to_all(parts, "y", 0, 0, tiled=True)
    result = merge(parts)
    return lax.ppermute(result, ALL, [(b, a) for a, b in query_moves()])


def solution(mesh):
    fine = Mesh(mesh.devices.reshape(8, 4, 2, 8), ALL)
    ctx = ("y", "x", "c")
    return jax.shard_map(
        body,
        mesh=fine,
        in_specs=(P(ctx, "z"), P(ctx, "z"), P("z", ctx)),
        out_specs=P("z", ctx),
        check_vma=False,
    )
```

```python
import jax
import jax.numpy as jnp
from jax import lax
from jax.experimental import pallas as pl
from jax.experimental.pallas import tpu as pltpu
from jax.sharding import Mesh, PartitionSpec as P

HD = 128
NT = (((1,), (1,)), ((), ()))
NN = (((1,), (0,)), ((), ()))


def spread(value, axis):
    count = lax.axis_size(axis)
    copies = jnp.broadcast_to(value[None], (count,) + value.shape)
    return lax.all_to_all(copies, axis, 0, 0, tiled=True)


def place(y, x, c, z):
    return ((y * 4 + x) * 2 + c) * 8 + z


def weight_moves():
    moves = []
    for y in range(8):
        for x in range(4):
            for c in range(2):
                shard = y * 8 + x * 2 + c
                kind, head, quarter = shard // 32, shard // 4 % 8, shard % 4
                for z in range(8):
                    target = place(kind * 4 + quarter, z // 2, z % 2, (head + 4) % 8)
                    moves.append((place(y, x, c, z), target))
    return moves


def query_moves():
    return [
        (place(y, x, c, z), place(z, x, c, (y + 4) % 8))
        for y in range(8)
        for x in range(4)
        for c in range(2)
        for z in range(8)
    ]


ALL = ("y", "x", "c", "z")
def shift(count, away):
    return [(i, (i + away) % count) for i in range(count)]


SWAP = [(0, 1), (1, 0)]


def project_kernel(mem_ref, own, left, right, opp, own_s, left_s, right_s, opp_s, out_ref):
    x, core = lax.axis_index("x"), lax.axis_index("c")
    pairs = []
    for half, refs in ((core, (own, left, right, opp)), (1 - core, (own_s, left_s, right_s, opp_s))):
        for away, ref in zip((0, 3, 1, 2), refs):
            pairs.append((2 * lax.rem(x + away, 4) + half, ref))
    total = None
    for share, ref in pairs:
        part = lax.dot_general(mem_ref[share], ref[...], NT, preferred_element_type=jnp.float32)
        total = part if total is None else total + part
    out_ref[...] = total.astype(out_ref.dtype)


def project(mem_all, *w_pieces):
    return pl.pallas_call(
        project_kernel,
        out_shape=jax.ShapeDtypeStruct((256, 2 * HD), jnp.bfloat16),
        compiler_params=pltpu.CompilerParams(vmem_limit_bytes=16 << 20),
        cost_estimate=pl.CostEstimate(flops=2 * 256 * 256 * 8192, bytes_accessed=8 << 20, transcendentals=0),
    )(mem_all, *w_pieces)


def attend_kernel(q_ref, own, other, out_ref):
    blocks = [(ref, start) for ref in (own, other) for start in range(0, 1024, 256)]
    query = q_ref[...]
    top = total = acc = None
    for ref, start in blocks:
        keys = ref[start : start + 256, :HD]
        values = ref[start : start + 256, HD:]
        scores = lax.dot_general(query, keys, NT, preferred_element_type=jnp.float32) * HD ** (-0.5)
        block_max = jnp.max(scores, axis=1, keepdims=True)
        expo = jnp.exp(scores - block_max)
        block_total = jnp.sum(expo, axis=1, keepdims=True)
        block_out = lax.dot_general(expo.astype(jnp.bfloat16), values, NN, preferred_element_type=jnp.float32)
        if top is None:
            top, total, acc = block_max, block_total, block_out
        else:
            new_top = jnp.maximum(top, block_max)
            keep, add = jnp.exp(top - new_top), jnp.exp(block_max - new_top)
            total = total * keep + block_total * add
            acc = acc * keep + block_out * add
            top = new_top
    tops = jnp.concatenate([top[h * 64 : h * 64 + 64] for h in range(8)], axis=1)
    totals = jnp.concatenate([total[h * 64 : h * 64 + 64] for h in range(8)], axis=1)
    stats = jnp.concatenate([tops, totals], axis=0).T
    for h in range(8):
        out_ref[h, :64, :] = acc[h * 64 : h * 64 + 64]
        out_ref[h, 64:, :] = jnp.broadcast_to(stats[h : h + 1], (8, HD))


def attend(query, own, other):
    return pl.pallas_call(
        attend_kernel,
        out_shape=jax.ShapeDtypeStruct((8, 72, HD), jnp.float32),
        compiler_params=pltpu.CompilerParams(vmem_limit_bytes=24 << 20),
        cost_estimate=pl.CostEstimate(
            flops=4 * 512 * 2048 * HD, bytes_accessed=2 << 20, transcendentals=512 * 2048
        ),
    )(query, own, other)


def merge_kernel(part_ref, out_ref):
    stats = jnp.concatenate([part_ref[j, 64:65, :] for j in range(8)], axis=0).T
    tops, totals = stats[:64], stats[64:]
    top = jnp.max(tops, axis=1, keepdims=True)
    factor = jnp.exp(tops - top)
    denom = jnp.sum(factor * totals, axis=1, keepdims=True)
    numer = factor[:, :1] * part_ref[0, :64, :]
    for j in range(1, 8):
        numer += factor[:, j : j + 1] * part_ref[j, :64, :]
    out_ref[...] = (numer / denom).astype(out_ref.dtype)


def merge(parts):
    return pl.pallas_call(
        merge_kernel,
        out_shape=jax.ShapeDtypeStruct((64, HD), jnp.bfloat16),
    )(parts)


def ring(value):
    half = value.shape[0] // 2
    left = lax.ppermute(value, "x", shift(4, 1))
    right = lax.ppermute(value, "x", shift(4, -1))
    opp_a = lax.ppermute(left[:half], "x", shift(4, 1))
    opp_b = lax.ppermute(right[half:], "x", shift(4, -1))
    return value, left, right, opp_a, opp_b


def swap(value):
    return lax.ppermute(value, "c", SWAP)


def body(memory, kv_weight, queries):
    mem_all = lax.all_gather(memory, "z", axis=0)
    rows = lax.ppermute(kv_weight, ALL, weight_moves())
    query = lax.ppermute(queries, ALL, query_moves())
    both = spread(jnp.concatenate([rows, query.reshape(8, 8 * HD)], axis=0), "y")
    rows = both[:, :32].reshape(2 * HD, 8 * HD)
    query = both[:, 32:].reshape(512, HD)
    rows, left, right, opp_k, opp_v = ring(rows)
    opp_k, opp_v, mem_all = lax.optimization_barrier((opp_k, opp_v, mem_all))
    opp = jnp.concatenate([opp_k, opp_v], axis=0)
    own = project(mem_all, rows, left, right, opp, swap(rows), swap(left), swap(right), swap(opp))

    own = lax.all_gather(own, "x", axis=0, tiled=True)
    parts = attend(query, own, swap(own))
    parts = lax.all_to_all(parts, "y", 0, 0, tiled=True)
    result = merge(parts)
    return lax.ppermute(result, ALL, [(b, a) for a, b in query_moves()])


def solution(mesh):
    fine = Mesh(mesh.devices.reshape(8, 4, 2, 8), ALL)
    ctx = ("y", "x", "c")
    return jax.shard_map(
        body,
        mesh=fine,
        in_specs=(P(ctx, "z"), P(ctx, "z"), P("z", ctx)),
        out_specs=P("z", ctx),
        check_vma=False,
    )
```

```python
import functools

import jax
import jax.numpy as jnp
from jax import lax
from jax.experimental import pallas as pl
from jax.experimental.pallas import tpu as pltpu
from jax.sharding import Mesh, PartitionSpec as P

HD = 128
NT = (((1,), (1,)), ((), ()))
NN = (((1,), (0,)), ((), ()))


def spread(value, axis):
    count = lax.axis_size(axis)
    copies = jnp.broadcast_to(value[None], (count,) + value.shape)
    return lax.all_to_all(copies, axis, 0, 0, tiled=True)


def place(y, x, c, z):
    return ((y * 4 + x) * 2 + c) * 8 + z


def weight_moves():
    moves = []
    for y in range(8):
        for x in range(4):
            for c in range(2):
                shard = y * 8 + x * 2 + c
                kind, head, quarter = shard // 32, shard // 4 % 8, shard % 4
                for z in range(8):
                    target = place(kind * 4 + quarter, z // 2, z % 2, (head + 4) % 8)
                    moves.append((place(y, x, c, z), target))
    return moves


def query_moves():
    return [
        (place(y, x, c, z), place(z, x, c, (y + 4) % 8))
        for y in range(8)
        for x in range(4)
        for c in range(2)
        for z in range(8)
    ]


ALL = ("y", "x", "c", "z")
def shift(count, away):
    return [(i, (i + away) % count) for i in range(count)]


SWAP = [(0, 1), (1, 0)]


def project_kernel(swapped, mem_ref, own, left, right, opp, *refs):
    x, core = lax.axis_index("x"), lax.axis_index("c")
    half = 1 - core if swapped else core
    *before, out_ref = refs
    total = before[0][...] if before else None
    for away, ref in zip((0, 3, 1, 2), (own, left, right, opp)):
        share = mem_ref[2 * lax.rem(x + away, 4) + half]
        part = lax.dot_general(share, ref[...], NT, preferred_element_type=jnp.float32)
        total = part if total is None else total + part
    out_ref[...] = total.astype(out_ref.dtype)


def project(dtype, mem_all, *operands):
    return pl.pallas_call(
        functools.partial(project_kernel, dtype == jnp.bfloat16),
        out_shape=jax.ShapeDtypeStruct((256, 2 * HD), dtype),
        compiler_params=pltpu.CompilerParams(vmem_limit_bytes=16 << 20),
        cost_estimate=pl.CostEstimate(flops=256 * 256 * 8192, bytes_accessed=4 << 20, transcendentals=0),
    )(mem_all, *operands)


def attend_kernel(q_ref, own, other, out_ref):
    blocks = [(ref, start) for ref in (own, other) for start in range(0, 1024, 256)]
    query = q_ref[...]
    top = total = acc = None
    for ref, start in blocks:
        keys = ref[start : start + 256, :HD]
        values = ref[start : start + 256, HD:]
        scores = lax.dot_general(query, keys, NT, preferred_element_type=jnp.float32) * HD ** (-0.5)
        block_max = jnp.max(scores, axis=1, keepdims=True)
        expo = jnp.exp(scores - block_max)
        block_total = jnp.sum(expo, axis=1, keepdims=True)
        block_out = lax.dot_general(expo.astype(jnp.bfloat16), values, NN, preferred_element_type=jnp.float32)
        if top is None:
            top, total, acc = block_max, block_total, block_out
        else:
            new_top = jnp.maximum(top, block_max)
            keep, add = jnp.exp(top - new_top), jnp.exp(block_max - new_top)
            total = total * keep + block_total * add
            acc = acc * keep + block_out * add
            top = new_top
    tops = jnp.concatenate([top[h * 64 : h * 64 + 64] for h in range(8)], axis=1)
    totals = jnp.concatenate([total[h * 64 : h * 64 + 64] for h in range(8)], axis=1)
    stats = jnp.concatenate([tops, totals], axis=0).T
    for h in range(8):
        out_ref[h, :64, :] = acc[h * 64 : h * 64 + 64]
        out_ref[h, 64:, :] = jnp.broadcast_to(stats[h : h + 1], (8, HD))


def attend(query, own, other):
    return pl.pallas_call(
        attend_kernel,
        out_shape=jax.ShapeDtypeStruct((8, 72, HD), jnp.float32),
        compiler_params=pltpu.CompilerParams(vmem_limit_bytes=24 << 20),
        cost_estimate=pl.CostEstimate(
            flops=4 * 512 * 2048 * HD, bytes_accessed=2 << 20, transcendentals=512 * 2048
        ),
    )(query, own, other)


def merge_kernel(part_ref, out_ref):
    stats = jnp.concatenate([part_ref[j, 64:65, :] for j in range(8)], axis=0).T
    tops, totals = stats[:64], stats[64:]
    top = jnp.max(tops, axis=1, keepdims=True)
    factor = jnp.exp(tops - top)
    denom = jnp.sum(factor * totals, axis=1, keepdims=True)
    numer = factor[:, :1] * part_ref[0, :64, :]
    for j in range(1, 8):
        numer += factor[:, j : j + 1] * part_ref[j, :64, :]
    out_ref[...] = (numer / denom).astype(out_ref.dtype)


def merge(parts):
    return pl.pallas_call(
        merge_kernel,
        out_shape=jax.ShapeDtypeStruct((64, HD), jnp.bfloat16),
    )(parts)


def ring(value):
    half = value.shape[0] // 2
    left = lax.ppermute(value, "x", shift(4, 1))
    right = lax.ppermute(value, "x", shift(4, -1))
    opp_a = lax.ppermute(left[:half], "x", shift(4, 1))
    opp_b = lax.ppermute(right[half:], "x", shift(4, -1))
    return value, left, right, opp_a, opp_b


def swap(value):
    return lax.ppermute(value, "c", SWAP)


def body(memory, kv_weight, queries):
    mem_all = lax.all_gather(memory, "z", axis=0)
    rows = lax.ppermute(kv_weight, ALL, weight_moves())
    query = lax.ppermute(queries, ALL, query_moves())
    both = spread(jnp.concatenate([rows, query.reshape(8, 8 * HD)], axis=0), "y")
    rows = both[:, :32].reshape(2 * HD, 8 * HD)
    query = both[:, 32:].reshape(512, HD)
    rows, left, right, opp_k, opp_v = ring(rows)
    opp_k, opp_v, mem_all = lax.optimization_barrier((opp_k, opp_v, mem_all))
    opp = jnp.concatenate([opp_k, opp_v], axis=0)
    near = project(jnp.float32, mem_all, rows, left, right, opp)
    own = project(jnp.bfloat16, mem_all, swap(rows), swap(left), swap(right), swap(opp), near)

    own = lax.all_gather(own, "x", axis=0, tiled=True)
    parts = attend(query, own, swap(own))
    parts = lax.all_to_all(parts, "y", 0, 0, tiled=True)
    result = merge(parts)
    return lax.ppermute(result, ALL, [(b, a) for a, b in query_moves()])


def solution(mesh):
    fine = Mesh(mesh.devices.reshape(8, 4, 2, 8), ALL)
    ctx = ("y", "x", "c")
    return jax.shard_map(
        body,
        mesh=fine,
        in_specs=(P(ctx, "z"), P(ctx, "z"), P("z", ctx)),
        out_specs=P("z", ctx),
        check_vma=False,
    )
```

```python
import functools

import jax
import jax.numpy as jnp
from jax import lax
from jax.experimental import pallas as pl
from jax.experimental.pallas import tpu as pltpu
from jax.sharding import Mesh, PartitionSpec as P

HD = 128
NT = (((1,), (1,)), ((), ()))
NN = (((1,), (0,)), ((), ()))


def spread(value, axis):
    count = lax.axis_size(axis)
    copies = jnp.broadcast_to(value[None], (count,) + value.shape)
    return lax.all_to_all(copies, axis, 0, 0, tiled=True)


def place(y, x, c, z):
    return ((y * 4 + x) * 2 + c) * 8 + z


def weight_moves():
    moves = []
    for y in range(8):
        for x in range(4):
            for c in range(2):
                shard = y * 8 + x * 2 + c
                kind, head, quarter = shard // 32, shard // 4 % 8, shard % 4
                for z in range(8):
                    target = place(kind * 4 + quarter, z // 2, z % 2, (head + 4) % 8)
                    moves.append((place(y, x, c, z), target))
    return moves


def query_moves():
    return [
        (place(y, x, c, z), place(z, x, c, (y + 4) % 8))
        for y in range(8)
        for x in range(4)
        for c in range(2)
        for z in range(8)
    ]


ALL = ("y", "x", "c", "z")
def shift(count, away):
    return [(i, (i + away) % count) for i in range(count)]


SWAP = [(0, 1), (1, 0)]


def project_kernel(swapped, mem_ref, own, left, right, opp, *refs):
    x, core = lax.axis_index("x"), lax.axis_index("c")
    half = 1 - core if swapped else core
    *before, out_ref = refs
    total = before[0][...] if before else None
    for away, ref in zip((0, 3, 1, 2), (own, left, right, opp)):
        share = mem_ref[2 * lax.rem(x + away, 4) + half]
        part = lax.dot_general(share, ref[...], NT, preferred_element_type=jnp.float32)
        total = part if total is None else total + part
    out_ref[...] = total.astype(out_ref.dtype)


def project(dtype, mem_all, *operands):
    return pl.pallas_call(
        functools.partial(project_kernel, dtype == jnp.bfloat16),
        out_shape=jax.ShapeDtypeStruct((256, 2 * HD), dtype),
        compiler_params=pltpu.CompilerParams(vmem_limit_bytes=16 << 20),
        cost_estimate=pl.CostEstimate(flops=256 * 256 * 8192, bytes_accessed=4 << 20, transcendentals=0),
    )(mem_all, *operands)


def attend_kernel(q_ref, own, other, out_ref):
    blocks = [(ref, start) for ref in (own, other) for start in range(0, 1024, 256)]
    query = q_ref[...]
    top = total = acc = None
    for ref, start in blocks:
        keys = ref[start : start + 256, :HD]
        values = ref[start : start + 256, HD:]
        scores = lax.dot_general(query, keys, NT, preferred_element_type=jnp.float32) * HD ** (-0.5)
        block_max = jnp.max(scores, axis=1, keepdims=True)
        expo = jnp.exp(scores - block_max)
        block_total = jnp.sum(expo, axis=1, keepdims=True)
        block_out = lax.dot_general(expo.astype(jnp.bfloat16), values, NN, preferred_element_type=jnp.float32)
        if top is None:
            top, total, acc = block_max, block_total, block_out
        else:
            new_top = jnp.maximum(top, block_max)
            keep, add = jnp.exp(top - new_top), jnp.exp(block_max - new_top)
            total = total * keep + block_total * add
            acc = acc * keep + block_out * add
            top = new_top
    tops = jnp.concatenate([top[h * 64 : h * 64 + 64] for h in range(8)], axis=1)
    totals = jnp.concatenate([total[h * 64 : h * 64 + 64] for h in range(8)], axis=1)
    stats = jnp.concatenate([tops, totals], axis=0).T
    for h in range(8):
        out_ref[h, :64, :] = acc[h * 64 : h * 64 + 64]
        out_ref[h, 64:, :] = jnp.broadcast_to(stats[h : h + 1], (8, HD))


def attend(query, own, other):
    return pl.pallas_call(
        attend_kernel,
        out_shape=jax.ShapeDtypeStruct((8, 72, HD), jnp.float32),
        compiler_params=pltpu.CompilerParams(vmem_limit_bytes=24 << 20),
        cost_estimate=pl.CostEstimate(
            flops=4 * 512 * 2048 * HD, bytes_accessed=2 << 20, transcendentals=512 * 2048
        ),
    )(query, own, other)


def merge_kernel(part_ref, out_ref):
    stats = jnp.concatenate([part_ref[j, 64:65, :] for j in range(8)], axis=0).T
    tops, totals = stats[:64], stats[64:]
    top = jnp.max(tops, axis=1, keepdims=True)
    factor = jnp.exp(tops - top)
    denom = jnp.sum(factor * totals, axis=1, keepdims=True)
    numer = factor[:, :1] * part_ref[0, :64, :]
    for j in range(1, 8):
        numer += factor[:, j : j + 1] * part_ref[j, :64, :]
    out_ref[...] = (numer / denom).astype(out_ref.dtype)


def merge(parts):
    return pl.pallas_call(
        merge_kernel,
        out_shape=jax.ShapeDtypeStruct((64, HD), jnp.bfloat16),
    )(parts)


def ring(value):
    half = value.shape[0] // 2
    left = lax.ppermute(value, "x", shift(4, 1))
    right = lax.ppermute(value, "x", shift(4, -1))
    swapped = swap(value)
    opp_a = lax.ppermute(left[:half], "x", shift(4, 1))
    opp_b = lax.ppermute(right[half:], "x", shift(4, -1))
    left, right, swapped = lax.optimization_barrier((left, right, swapped))
    return swapped, left, right, opp_a, opp_b


def swap(value):
    return lax.ppermute(value, "c", SWAP)


def body(memory, kv_weight, queries):
    mem_all = lax.all_gather(memory, "z", axis=0)
    rows = lax.ppermute(kv_weight, ALL, weight_moves())
    query = lax.ppermute(queries, ALL, query_moves())
    both = spread(jnp.concatenate([rows, query.reshape(8, 8 * HD)], axis=0), "y")
    rows = both[:, :32].reshape(2 * HD, 8 * HD)
    query = both[:, 32:].reshape(512, HD)
    rows_s, left, right, opp_k, opp_v = ring(rows)
    opp_k, opp_v, mem_all = lax.optimization_barrier((opp_k, opp_v, mem_all))
    opp = jnp.concatenate([opp_k, opp_v], axis=0)
    near = project(jnp.float32, mem_all, rows, left, right, opp)
    own = project(jnp.bfloat16, mem_all, rows_s, swap(left), swap(right), swap(opp), near)

    own = lax.all_gather(own, "x", axis=0, tiled=True)
    parts = attend(query, own, swap(own))
    parts = lax.all_to_all(parts, "y", 0, 0, tiled=True)
    result = merge(parts)
    return lax.ppermute(result, ALL, [(b, a) for a, b in query_moves()])


def solution(mesh):
    fine = Mesh(mesh.devices.reshape(8, 4, 2, 8), ALL)
    ctx = ("y", "x", "c")
    return jax.shard_map(
        body,
        mesh=fine,
        in_specs=(P(ctx, "z"), P(ctx, "z"), P("z", ctx)),
        out_specs=P("z", ctx),
        check_vma=False,
    )
```

```python
import functools

import jax
import jax.numpy as jnp
from jax import lax
from jax.experimental import pallas as pl
from jax.experimental.pallas import tpu as pltpu
from jax.sharding import Mesh, PartitionSpec as P

HD = 128
NT = (((1,), (1,)), ((), ()))
NN = (((1,), (0,)), ((), ()))


def spread(value, axis):
    count = lax.axis_size(axis)
    copies = jnp.broadcast_to(value[None], (count,) + value.shape)
    return lax.all_to_all(copies, axis, 0, 0, tiled=True)


def place(y, x, c, z):
    return ((y * 4 + x) * 2 + c) * 8 + z


def weight_moves():
    moves = []
    for y in range(8):
        for x in range(4):
            for c in range(2):
                shard = y * 8 + x * 2 + c
                kind, head, quarter = shard // 32, shard // 4 % 8, shard % 4
                for z in range(8):
                    target = place(kind * 4 + quarter, z // 2, z % 2, (head + 4) % 8)
                    moves.append((place(y, x, c, z), target))
    return moves


def query_moves():
    return [
        (place(y, x, c, z), place(z, x, c, (y + 4) % 8))
        for y in range(8)
        for x in range(4)
        for c in range(2)
        for z in range(8)
    ]


ALL = ("y", "x", "c", "z")
def shift(count, away):
    return [(i, (i + away) % count) for i in range(count)]


SWAP = [(0, 1), (1, 0)]


def project_kernel(swapped, mem_ref, own, left, right, opp, *refs):
    x, core = lax.axis_index("x"), lax.axis_index("c")
    half = 1 - core if swapped else core
    *before, out_ref = refs
    total = before[0][...] if before else None
    for away, ref in zip((0, 3, 1, 2), (own, left, right, opp)):
        share = mem_ref[2 * lax.rem(x + away, 4) + half]
        part = lax.dot_general(share, ref[...], NT, preferred_element_type=jnp.float32)
        total = part if total is None else total + part
    out_ref[...] = total.astype(out_ref.dtype)


def project(dtype, mem_all, *operands):
    return pl.pallas_call(
        functools.partial(project_kernel, dtype == jnp.bfloat16),
        out_shape=jax.ShapeDtypeStruct((256, 2 * HD), dtype),
        compiler_params=pltpu.CompilerParams(vmem_limit_bytes=16 << 20),
        cost_estimate=pl.CostEstimate(flops=256 * 256 * 8192, bytes_accessed=4 << 20, transcendentals=0),
    )(mem_all, *operands)


def attend_kernel(q_ref, own, other, out_ref):
    blocks = [(ref, start) for ref in (own, other) for start in range(0, 1024, 256)]
    query = q_ref[...]
    top = total = acc = None
    for ref, start in blocks:
        keys = ref[start : start + 256, :HD]
        values = ref[start : start + 256, HD:]
        scores = lax.dot_general(query, keys, NT, preferred_element_type=jnp.float32) * HD ** (-0.5)
        block_max = jnp.max(scores, axis=1, keepdims=True)
        expo = jnp.exp(scores - block_max)
        block_total = jnp.sum(expo, axis=1, keepdims=True)
        block_out = lax.dot_general(expo.astype(jnp.bfloat16), values, NN, preferred_element_type=jnp.float32)
        if top is None:
            top, total, acc = block_max, block_total, block_out
        else:
            new_top = jnp.maximum(top, block_max)
            keep, add = jnp.exp(top - new_top), jnp.exp(block_max - new_top)
            total = total * keep + block_total * add
            acc = acc * keep + block_out * add
            top = new_top
    tops = jnp.concatenate([top[h * 64 : h * 64 + 64] for h in range(8)], axis=1)
    totals = jnp.concatenate([total[h * 64 : h * 64 + 64] for h in range(8)], axis=1)
    stats = jnp.concatenate([tops, totals], axis=0).T
    for h in range(8):
        out_ref[h, :64, :] = acc[h * 64 : h * 64 + 64]
        out_ref[h, 64:, :] = jnp.broadcast_to(stats[h : h + 1], (8, HD))


def attend(query, own, other):
    return pl.pallas_call(
        attend_kernel,
        out_shape=jax.ShapeDtypeStruct((8, 72, HD), jnp.float32),
        compiler_params=pltpu.CompilerParams(vmem_limit_bytes=24 << 20),
        cost_estimate=pl.CostEstimate(
            flops=4 * 512 * 2048 * HD, bytes_accessed=2 << 20, transcendentals=512 * 2048
        ),
    )(query, own, other)


def merge_kernel(part_ref, out_ref):
    stats = jnp.concatenate([part_ref[j, 64:65, :] for j in range(8)], axis=0).T
    tops, totals = stats[:64], stats[64:]
    top = jnp.max(tops, axis=1, keepdims=True)
    factor = jnp.exp(tops - top)
    denom = jnp.sum(factor * totals, axis=1, keepdims=True)
    numer = factor[:, :1] * part_ref[0, :64, :]
    for j in range(1, 8):
        numer += factor[:, j : j + 1] * part_ref[j, :64, :]
    out_ref[...] = (numer / denom).astype(out_ref.dtype)


def merge(parts):
    return pl.pallas_call(
        merge_kernel,
        out_shape=jax.ShapeDtypeStruct((64, HD), jnp.bfloat16),
    )(parts)


def ring(value):
    half = value.shape[0] // 2
    left = lax.ppermute(value, "x", shift(4, 1))
    right = lax.ppermute(value, "x", shift(4, -1))
    swapped = swap(value)
    opp_a = lax.ppermute(left[:half], "x", shift(4, 1))
    opp_b = lax.ppermute(right[half:], "x", shift(4, -1))
    left, right, swapped = lax.optimization_barrier((left, right, swapped))
    return swapped, left, right, opp_a, opp_b


def swap(value):
    return lax.ppermute(value, "c", SWAP)


def body(memory, kv_weight, queries):
    mem_all = lax.all_gather(memory, "z", axis=0)
    rows = lax.ppermute(kv_weight, ALL, weight_moves())
    query = lax.ppermute(queries, ALL, query_moves())
    both = spread(jnp.concatenate([rows, query.reshape(8, 8 * HD)], axis=0), "y")
    rows = both[:, :32].reshape(2 * HD, 8 * HD)
    query = both[:, 32:].reshape(512, HD)
    rows_s, left, right, opp_k, opp_v = ring(rows)
    opp_k, opp_v, mem_all = lax.optimization_barrier((opp_k, opp_v, mem_all))
    opp = jnp.concatenate([opp_k, opp_v], axis=0)
    near = project(jnp.float32, mem_all, rows, left, right, opp)
    own = project(jnp.bfloat16, mem_all, rows_s, swap(left), swap(right), swap(opp), near)

    own = spread(own, "x").reshape(1024, 2 * HD)
    parts = attend(query, own, swap(own))
    parts = lax.all_to_all(parts, "y", 0, 0, tiled=True)
    result = merge(parts)
    return lax.ppermute(result, ALL, [(b, a) for a, b in query_moves()])


def solution(mesh):
    fine = Mesh(mesh.devices.reshape(8, 4, 2, 8), ALL)
    ctx = ("y", "x", "c")
    return jax.shard_map(
        body,
        mesh=fine,
        in_specs=(P(ctx, "z"), P(ctx, "z"), P("z", ctx)),
        out_specs=P("z", ctx),
        check_vma=False,
    )
```

```python
import functools

import jax
import jax.numpy as jnp
from jax import lax
from jax.experimental import pallas as pl
from jax.experimental.pallas import tpu as pltpu
from jax.sharding import Mesh, PartitionSpec as P

HD = 128
NT = (((1,), (1,)), ((), ()))
NN = (((1,), (0,)), ((), ()))


def spread(value, axis):
    count = lax.axis_size(axis)
    copies = jnp.broadcast_to(value[None], (count,) + value.shape)
    return lax.all_to_all(copies, axis, 0, 0, tiled=True)


def place(y, x, c, z):
    return ((y * 4 + x) * 2 + c) * 8 + z


def weight_moves():
    moves = []
    for y in range(8):
        for x in range(4):
            for c in range(2):
                shard = y * 8 + x * 2 + c
                kind, head, quarter = shard // 32, shard // 4 % 8, shard % 4
                for z in range(8):
                    target = place(kind * 4 + quarter, z // 2, z % 2, (head + 4) % 8)
                    moves.append((place(y, x, c, z), target))
    return moves


def query_moves():
    return [
        (place(y, x, c, z), place(z, x, c, (y + 4) % 8))
        for y in range(8)
        for x in range(4)
        for c in range(2)
        for z in range(8)
    ]


ALL = ("y", "x", "c", "z")
def shift(count, away):
    return [(i, (i + away) % count) for i in range(count)]


SWAP = [(0, 1), (1, 0)]


def project_kernel(swapped, mem_ref, own, left, right, opp_k, opp_v, *refs):
    x, core = lax.axis_index("x"), lax.axis_index("c")
    half = 1 - core if swapped else core
    *before, out_ref = refs
    total = before[0][...] if before else None
    opp = jnp.concatenate([opp_k[...], opp_v[...]], axis=0)
    for away, rows in zip((0, 3, 1, 2), (own[...], left[...], right[...], opp)):
        share = mem_ref[2 * lax.rem(x + away, 4) + half]
        part = lax.dot_general(share, rows, NT, preferred_element_type=jnp.float32)
        total = part if total is None else total + part
    out_ref[...] = total.astype(out_ref.dtype)


def project(dtype, mem_all, *operands):
    return pl.pallas_call(
        functools.partial(project_kernel, dtype == jnp.bfloat16),
        out_shape=jax.ShapeDtypeStruct((256, 2 * HD), dtype),
        compiler_params=pltpu.CompilerParams(vmem_limit_bytes=16 << 20),
        cost_estimate=pl.CostEstimate(flops=256 * 256 * 8192, bytes_accessed=4 << 20, transcendentals=0),
    )(mem_all, *operands)


def attend_kernel(q_ref, own, other, out_ref):
    blocks = [(ref, start) for ref in (own, other) for start in range(0, 1024, 256)]
    query = q_ref[...]
    top = total = acc = None
    for ref, start in blocks:
        keys = ref[start : start + 256, :HD]
        values = ref[start : start + 256, HD:]
        scores = lax.dot_general(query, keys, NT, preferred_element_type=jnp.float32) * HD ** (-0.5)
        block_max = jnp.max(scores, axis=1, keepdims=True)
        expo = jnp.exp(scores - block_max)
        block_total = jnp.sum(expo, axis=1, keepdims=True)
        block_out = lax.dot_general(expo.astype(jnp.bfloat16), values, NN, preferred_element_type=jnp.float32)
        if top is None:
            top, total, acc = block_max, block_total, block_out
        else:
            new_top = jnp.maximum(top, block_max)
            keep, add = jnp.exp(top - new_top), jnp.exp(block_max - new_top)
            total = total * keep + block_total * add
            acc = acc * keep + block_out * add
            top = new_top
    tops = jnp.concatenate([top[h * 64 : h * 64 + 64] for h in range(8)], axis=1)
    totals = jnp.concatenate([total[h * 64 : h * 64 + 64] for h in range(8)], axis=1)
    stats = jnp.concatenate([tops, totals], axis=0).T
    for h in range(8):
        out_ref[h, :64, :] = acc[h * 64 : h * 64 + 64]
        out_ref[h, 64:, :] = jnp.broadcast_to(stats[h : h + 1], (8, HD))


def attend(query, own, other):
    return pl.pallas_call(
        attend_kernel,
        out_shape=jax.ShapeDtypeStruct((8, 72, HD), jnp.float32),
        compiler_params=pltpu.CompilerParams(vmem_limit_bytes=24 << 20),
        cost_estimate=pl.CostEstimate(
            flops=4 * 512 * 2048 * HD, bytes_accessed=2 << 20, transcendentals=512 * 2048
        ),
    )(query, own, other)


def merge_kernel(part_ref, out_ref):
    stats = jnp.concatenate([part_ref[j, 64:65, :] for j in range(8)], axis=0).T
    tops, totals = stats[:64], stats[64:]
    top = jnp.max(tops, axis=1, keepdims=True)
    factor = jnp.exp(tops - top)
    denom = jnp.sum(factor * totals, axis=1, keepdims=True)
    numer = factor[:, :1] * part_ref[0, :64, :]
    for j in range(1, 8):
        numer += factor[:, j : j + 1] * part_ref[j, :64, :]
    out_ref[...] = (numer / denom).astype(out_ref.dtype)


def merge(parts):
    return pl.pallas_call(
        merge_kernel,
        out_shape=jax.ShapeDtypeStruct((64, HD), jnp.bfloat16),
    )(parts)


def ring(value):
    half = value.shape[0] // 2
    left = lax.ppermute(value, "x", shift(4, 1))
    right = lax.ppermute(value, "x", shift(4, -1))
    swapped = swap(value)
    opp_a = lax.ppermute(left[:half], "x", shift(4, 1))
    opp_b = lax.ppermute(right[half:], "x", shift(4, -1))
    left, right, swapped = lax.optimization_barrier((left, right, swapped))
    return swapped, left, right, opp_a, opp_b


def swap(value):
    return lax.ppermute(value, "c", SWAP)


def body(memory, kv_weight, queries):
    mem_all = lax.all_gather(memory, "z", axis=0)
    rows = lax.ppermute(kv_weight, ALL, weight_moves())
    query = lax.ppermute(queries, ALL, query_moves())
    both = spread(jnp.concatenate([rows, query.reshape(8, 8 * HD)], axis=0), "y")
    rows = both[:, :32].reshape(2 * HD, 8 * HD)
    query = both[:, 32:].reshape(512, HD)
    rows_s, left, right, opp_k, opp_v = ring(rows)
    opp_k, mem_all = lax.optimization_barrier((opp_k, mem_all))
    near = project(jnp.float32, mem_all, rows, left, right, opp_k, opp_v)
    swapped = [rows_s, *map(swap, (left, right, opp_k, opp_v))]
    own = project(jnp.bfloat16, mem_all, *swapped, near)

    own = spread(own, "x").reshape(1024, 2 * HD)
    parts = attend(query, own, swap(own))
    parts = lax.all_to_all(parts, "y", 0, 0, tiled=True)
    result = merge(parts)
    return lax.ppermute(result, ALL, [(b, a) for a, b in query_moves()])


def solution(mesh):
    fine = Mesh(mesh.devices.reshape(8, 4, 2, 8), ALL)
    ctx = ("y", "x", "c")
    return jax.shard_map(
        body,
        mesh=fine,
        in_specs=(P(ctx, "z"), P(ctx, "z"), P("z", ctx)),
        out_specs=P("z", ctx),
        check_vma=False,
    )
```

```python
import functools

import jax
import jax.numpy as jnp
from jax import lax
from jax.experimental import pallas as pl
from jax.experimental.pallas import tpu as pltpu
from jax.sharding import Mesh, PartitionSpec as P

HD = 128
NT = (((1,), (1,)), ((), ()))
NN = (((1,), (0,)), ((), ()))


def spread(value, axis):
    count = lax.axis_size(axis)
    copies = jnp.broadcast_to(value[None], (count,) + value.shape)
    return lax.all_to_all(copies, axis, 0, 0, tiled=True)


def place(y, x, c, z):
    return ((y * 4 + x) * 2 + c) * 8 + z


def weight_moves():
    moves = []
    for y in range(8):
        for x in range(4):
            for c in range(2):
                shard = y * 8 + x * 2 + c
                kind, head, quarter = shard // 32, shard // 4 % 8, shard % 4
                for z in range(8):
                    target = place(kind * 4 + quarter, z // 2, z % 2, (head + 4) % 8)
                    moves.append((place(y, x, c, z), target))
    return moves


def query_moves():
    return [
        (place(y, x, c, z), place(z, x, c, (y + 4) % 8))
        for y in range(8)
        for x in range(4)
        for c in range(2)
        for z in range(8)
    ]


ALL = ("y", "x", "c", "z")
def shift(count, away):
    return [(i, (i + away) % count) for i in range(count)]


SWAP = [(0, 1), (1, 0)]


def project_kernel(swapped, mem_ref, own, left, right, opp, *refs):
    x, core = lax.axis_index("x"), lax.axis_index("c")
    half = 1 - core if swapped else core
    *before, out_ref = refs
    total = before[0][...] if before else None
    for away, ref in zip((0, 3, 1, 2), (own, left, right, opp)):
        share = mem_ref[2 * lax.rem(x + away, 4) + half]
        part = lax.dot_general(share, ref[...], NT, preferred_element_type=jnp.float32)
        total = part if total is None else total + part
    out_ref[...] = total.astype(out_ref.dtype)


def project(dtype, mem_all, *operands):
    return pl.pallas_call(
        functools.partial(project_kernel, dtype == jnp.bfloat16),
        out_shape=jax.ShapeDtypeStruct((256, 2 * HD), dtype),
        compiler_params=pltpu.CompilerParams(vmem_limit_bytes=16 << 20),
        cost_estimate=pl.CostEstimate(flops=256 * 256 * 8192, bytes_accessed=4 << 20, transcendentals=0),
    )(mem_all, *operands)


def attend_kernel(q_ref, own, other, out_ref):
    blocks = [(ref, start) for ref in (own, other) for start in range(0, 1024, 256)]
    query = q_ref[...]
    top = total = acc = None
    for ref, start in blocks:
        keys = ref[start : start + 256, :HD]
        values = ref[start : start + 256, HD:]
        scores = lax.dot_general(query, keys, NT, preferred_element_type=jnp.float32) * HD ** (-0.5)
        block_max = jnp.max(scores, axis=1, keepdims=True)
        expo = jnp.exp(scores - block_max)
        block_total = jnp.sum(expo, axis=1, keepdims=True)
        block_out = lax.dot_general(expo.astype(jnp.bfloat16), values, NN, preferred_element_type=jnp.float32)
        if top is None:
            top, total, acc = block_max, block_total, block_out
        else:
            new_top = jnp.maximum(top, block_max)
            keep, add = jnp.exp(top - new_top), jnp.exp(block_max - new_top)
            total = total * keep + block_total * add
            acc = acc * keep + block_out * add
            top = new_top
    tops = jnp.concatenate([top[h * 64 : h * 64 + 64] for h in range(8)], axis=1)
    totals = jnp.concatenate([total[h * 64 : h * 64 + 64] for h in range(8)], axis=1)
    stats = jnp.concatenate([tops, totals], axis=0).T
    for h in range(8):
        out_ref[h, :64, :] = acc[h * 64 : h * 64 + 64]
        out_ref[h, 64:, :] = jnp.broadcast_to(stats[h : h + 1], (8, HD))


def attend(query, own, other):
    return pl.pallas_call(
        attend_kernel,
        out_shape=jax.ShapeDtypeStruct((8, 72, HD), jnp.float32),
        compiler_params=pltpu.CompilerParams(vmem_limit_bytes=24 << 20),
        cost_estimate=pl.CostEstimate(
            flops=4 * 512 * 2048 * HD, bytes_accessed=2 << 20, transcendentals=512 * 2048
        ),
    )(query, own, other)


def merge_kernel(part_ref, out_ref):
    stats = part_ref[:, 64, :].T
    tops, totals = stats[:64], stats[64:]
    top = jnp.max(tops, axis=1, keepdims=True)
    factor = jnp.exp(tops - top)
    denom = jnp.sum(factor * totals, axis=1, keepdims=True)
    numer = factor[:, :1] * part_ref[0, :64, :]
    for j in range(1, 8):
        numer += factor[:, j : j + 1] * part_ref[j, :64, :]
    out_ref[...] = (numer / denom).astype(out_ref.dtype)


def merge(parts):
    return pl.pallas_call(
        merge_kernel,
        out_shape=jax.ShapeDtypeStruct((64, HD), jnp.bfloat16),
    )(parts)


def ring(value):
    half = value.shape[0] // 2
    left = lax.ppermute(value, "x", shift(4, 1))
    right = lax.ppermute(value, "x", shift(4, -1))
    swapped = swap(value)
    opp_a = lax.ppermute(left[:half], "x", shift(4, 1))
    opp_b = lax.ppermute(right[half:], "x", shift(4, -1))
    left, right, swapped = lax.optimization_barrier((left, right, swapped))
    return swapped, left, right, opp_a, opp_b


def swap(value):
    return lax.ppermute(value, "c", SWAP)


def body(memory, kv_weight, queries):
    mem_all = lax.all_gather(memory, "z", axis=0)
    rows = lax.ppermute(kv_weight, ALL, weight_moves())
    query = lax.ppermute(queries, ALL, query_moves())
    both = spread(jnp.concatenate([rows, query.reshape(8, 8 * HD)], axis=0), "y")
    rows = both[:, :32].reshape(2 * HD, 8 * HD)
    query = both[:, 32:].reshape(512, HD)
    rows_s, left, right, opp_k, opp_v = ring(rows)
    opp_k, opp_v, mem_all = lax.optimization_barrier((opp_k, opp_v, mem_all))
    opp = jnp.concatenate([opp_k, opp_v], axis=0)
    near = project(jnp.float32, mem_all, rows, left, right, opp)
    own = project(jnp.bfloat16, mem_all, rows_s, swap(left), swap(right), swap(opp), near)

    own = spread(own, "x").reshape(1024, 2 * HD)
    parts = attend(query, own, swap(own))
    parts = lax.all_to_all(parts, "y", 0, 0, tiled=True)
    result = merge(parts)
    return lax.ppermute(result, ALL, [(b, a) for a, b in query_moves()])


def solution(mesh):
    fine = Mesh(mesh.devices.reshape(8, 4, 2, 8), ALL)
    ctx = ("y", "x", "c")
    return jax.shard_map(
        body,
        mesh=fine,
        in_specs=(P(ctx, "z"), P(ctx, "z"), P("z", ctx)),
        out_specs=P("z", ctx),
        check_vma=False,
    )
```
